32 devices in a mesh: dp: 4 (over y, core), shard: 8 (over z, x).
Axes of the slice: x: 2, y: 2, z: 4, core: 2. Of those that a mesh axis runs over, the one named last changes fastest.
Arguments:
- tokens: bfloat16 [32768, 768], P(('dp', 'shard')), may hold values from -6 to 6
- segment_ids: int32 [32768], P(('dp', 'shard')), may hold values from 0 to 127, never falling along the last dimension, each value on 1 to 512 neighbouring positions
- routes: int32 [32768, 2], P(('dp', 'shard')), may hold values from 0 to 3, all different within a row; in each aligned block of 1024 rows (0 to 1023, 1024 to 2047, ...) at most 640 rows name the same one
- buckets: int32 [1024], replicated, may hold values from 0 to 31, never falling along the last dimension, each value on 1 to 128 neighbouring positions
- norm1_gain: bfloat16 [768], P('shard'), may hold values from 0.5 to 1.5
- w_qkv: bfloat16 [768, 2304], P('shard'), may hold values from -0.21875 to 0.21875
- w_attn_out: bfloat16 [768, 768], P('shard'), may hold values from -0.875 to 0.875
- bias_table: bfloat16 [32, 12], P('shard'), may hold values from -4 to 4
- norm2_gain: bfloat16 [768], P('shard'), may hold values from 0.5 to 1.5
- router: bfloat16 [768, 4], P('shard'), may hold values from -0.15625 to 0.15625
- w_in: bfloat16 [4, 768, 3072], P(None, 'shard'), may hold values from -0.21875 to 0.21875
- w_expert_out: bfloat16 [4, 3072, 768], P(None, 'shard'), may hold values from -0.15625 to 0.15625
- cotangent: bfloat16 [32768, 768], P(('dp', 'shard')), may hold values from -6 to 6
Outputs:
- mixed_out: bfloat16 [32768, 768], P(('dp', 'shard'))
- grad_tokens: bfloat16 [32768, 768], P(('dp', 'shard'))
- grad_norm1: float32 [768], P('shard')
- grad_qkv: float32 [768, 2304], P('shard')
- grad_attn_out: float32 [768, 768], P('shard')
- grad_bias_table: float32 [32, 12], P('shard')
- grad_norm2: float32 [768], P('shard')
- grad_router: float32 [768, 4], P('shard')
- grad_w_in: float32 [4, 768, 3072], P(None, 'shard')
- grad_w_expert_out: float32 [4, 3072, 768], P(None, 'shard')
The draws below stay inside these ranges and needn't reach their ends.
Inputs may be any that keep to these rules, and one draw needn't show every extreme that they name: `routes`: each row names two different experts; among the rows of one device no expert is named more than 640 times, and in every draw some expert is named exactly 640 times by the rows of some device. `segment_ids`: never falling along the tokens; a document holds at most 1024 // 2 tokens. `buckets`: never falling with the distance.
All inputs are finite; a program needn't handle non-finite values.
Results may differ from the reference program's by a relative error of at most 0.023.
Values may be sent and summed in bfloat16 or wider, within the bound.
No kernel may reach another device: no remote copies, remote signals or barrier semaphores. Data moves between devices by JAX's collectives and lax.ppermute only.
A program may use at most 384 MiB of HBM per device.

```python
import math
import jax
import jax.numpy as jnp
import numpy as np
from jax import lax

D = 768
HEADS = 12
HEAD_DIM = 64
FF = 3072
EXPERTS = 4
BUCKETS = 32
SEQ = 1024
TOK_DEV = 1024
CAP = 640
TOKENS = 32768


def levels(key, shape, cuts, smallest, largest):
    gain, own = 1.0, jax.random.fold_in(key, 6)
    for dim, parts in cuts:
        draws = jnp.exp(jax.random.uniform(jax.random.fold_in(own, dim), (parts,), jnp.float32, smallest / len(cuts), largest / len(cuts)))
        gain = gain * jnp.repeat(draws, shape[dim] // parts).reshape([-1 if axis == dim else 1 for axis in range(len(shape))])
    return gain


def profile(count, total, limit, lean):
    loads = [(1 << 20) // math.isqrt(standing ** lean) + 1 for standing in range(2, count + 1)]
    surplus, counts = total - limit - (count - 1), [1] * (count - 1)
    while surplus > 0:
        candidates = [i for i in range(count - 1) if counts[i] < limit]
        pool, budget = sum([loads[i] for i in candidates]), surplus
        for i in candidates:
            addition = min(limit - counts[i], max(1, budget * loads[i] // pool), surplus)
            counts[i] = counts[i] + addition
            surplus = surplus - addition
    return np.array([limit] + counts)


def ragged_sizes(key, number_of, total, reach, lean):
    if number_of == 2:
        one = jax.random.randint(key, (), max(1, total - reach), min(reach, total - 1) + 1)
        return jnp.stack([one, total - one])
    tallies = jnp.asarray(profile(number_of, total, reach, lean), jnp.int32)
    pairs = (number_of - 1) // 2
    donor, sink = tallies[1:1 + 2 * pairs:2], tallies[2:2 + 2 * pairs:2]
    room = jnp.minimum(donor - 1, reach - sink)
    moved = jax.random.randint(jax.random.fold_in(key, 1), (pairs,), 0, 1 << 20) % (room + 1)
    tallies = tallies.at[1:1 + 2 * pairs:2].set(donor - moved).at[2:2 + 2 * pairs:2].set(sink + moved)
    return tallies[jax.random.permutation(jax.random.fold_in(key, 2), number_of)]


def deal_out(own_key, own, number, rows, amount, top, bound, slope):
    sequence = jax.random.permutation(own_key, amount)
    crowded, common = portions_of(amount, rows * top, bound, slope, True), portions_of(amount, rows * top, bound, slope, False)
    places = jnp.arange(amount)

    def named(tallies, rotation):
        used = int((tallies > 0).sum())
        fixed = max(1, used // 4)
        moved = fixed + (places - fixed + rotation * (used - fixed)) % max(1, amount - fixed)
        return jnp.zeros((amount,), jnp.int32).at[sequence[jnp.where(places < fixed, places, moved)]].set(jnp.asarray(tallies, jnp.int32))

    tallies = jnp.where(number % 4 == 0, named(crowded, number // 4), named(common, number - number // 4 - 1))
    mixed = jax.random.permutation(jax.random.fold_in(own, 3), amount)
    source_of, taker = mixed[0:amount // 2 * 2:2], mixed[1:amount // 2 * 2:2]
    room = jnp.minimum(tallies[source_of] - 1, bound - tallies[taker]) // 2
    room = jnp.where((source_of == sequence[0]) | (taker == sequence[0]) | (tallies[taker] == 0), 0, jnp.maximum(room, 0))
    moved = jax.random.randint(jax.random.fold_in(own, 4), (amount // 2,), 0, 1 << 20) % (room + 1)
    tallies = tallies.at[source_of].add(-moved).at[taker].add(moved)
    items = jnp.searchsorted(jnp.cumsum(tallies), jnp.arange(rows * top), side="right").astype(jnp.int32)
    grid = items.reshape(top, rows).T
    grid = grid[jax.random.permutation(jax.random.fold_in(own, 1), rows)]
    rotation = jax.random.randint(jax.random.fold_in(own, 2), (rows, 1), 0, top)
    return jnp.take_along_axis(grid, (jnp.arange(top)[None, :] + rotation) % top, axis=1)


def portions_of(number_of, total, limit, skew, full):
    weights = [(1 << 20) // math.isqrt(grade ** skew) + 1 for grade in range(1, number_of + 1)]
    largest = limit if full else min(limit, max(-(-total // number_of), total * weights[0] // sum(weights)))
    least = 1 if total - largest >= number_of - 1 else 0
    counts, surplus = [largest] + [least] * (number_of - 1), total - largest - least * (number_of - 1)
    while surplus > 0:
        movable = [i for i in range(1, number_of) if counts[i] < largest] or [i for i in range(1, number_of) if counts[i] < limit]
        pool, left = sum([weights[i] for i in movable]), surplus
        for i in movable:
            more = min(limit - counts[i], max(1, left * weights[i] // pool), surplus)
            counts[i] = counts[i] + more
            surplus = surplus - more
    return np.array(counts)


def bell_draw(own_key, extent, spread, limit, cuts=(), held_as=jnp.bfloat16):
    entries = spread * jax.random.normal(own_key, extent, jnp.float32)
    if cuts:
        entries = entries * levels(own_key, extent, cuts, -0.22, 0.18)
    return jnp.clip(entries, -limit, limit).astype(held_as)


def setup_inputs(seed: int = 0) -> dict:
    arg_keys = jax.random.split(jax.random.key(seed), 14)
    tokens = bell_draw(arg_keys[0], (TOKENS, D), 1.0, 6.0, ((0, 32),))
    segment_ids = jnp.searchsorted(jnp.cumsum(ragged_sizes(arg_keys[1], 4 * TOKENS // SEQ, TOKENS, SEQ // 2, 1)), jnp.arange(TOKENS), side="right").astype(jnp.int32)
    routes_keys = jax.random.split(jax.random.fold_in(arg_keys[2], 1), TOKENS // TOK_DEV)
    routes_turns = jax.random.permutation(jax.random.fold_in(arg_keys[2], 3), TOKENS // TOK_DEV)
    routes = jax.vmap(lambda own, number: deal_out(jax.random.fold_in(arg_keys[2], 2), own, number, TOK_DEV, EXPERTS, 2, CAP, 2))(routes_keys, routes_turns).reshape((TOKENS, 2))
    buckets = jnp.searchsorted(jnp.cumsum(ragged_sizes(arg_keys[3], BUCKETS, SEQ, SEQ // 8, 1)), jnp.arange(SEQ), side="right").astype(jnp.int32)
    norm1_gain = jnp.clip(1.0 + 0.1 * jax.random.normal(arg_keys[4], (D,), jnp.float32), 0.5, 1.5).astype(jnp.bfloat16)
    w_qkv = bell_draw(arg_keys[5], (D, 3 * D), D ** -0.5, 0.21875, ((0, 8),))
    w_attn_out = bell_draw(arg_keys[6], (D, D), (D // 16) ** -0.5, 0.875, ((0, 8),))
    bias_table = bell_draw(arg_keys[7], (BUCKETS, HEADS), 1.0, 4.0, ((0, 8),))
    norm2_gain = jnp.clip(1.0 + 0.1 * jax.random.normal(arg_keys[8], (D,), jnp.float32), 0.5, 1.5).astype(jnp.bfloat16)
    router = bell_draw(arg_keys[9], (D, EXPERTS), (2 * D) ** -0.5, 0.15625, ((0, 8),))
    w_in = bell_draw(arg_keys[10], (EXPERTS, D, FF), D ** -0.5, 0.21875, ((1, 8),))
    w_expert_out = bell_draw(arg_keys[11], (EXPERTS, FF, D), (FF // 2) ** -0.5, 0.15625, ((1, 8),))
    cotangent = bell_draw(arg_keys[12], (TOKENS, D), 1.0, 6.0, ((0, 32),))
    return {"tokens": tokens, "segment_ids": segment_ids, "routes": routes, "buckets": buckets, "norm1_gain": norm1_gain, "w_qkv": w_qkv, "w_attn_out": w_attn_out, "bias_table": bias_table, "norm2_gain": norm2_gain, "router": router, "w_in": w_in, "w_expert_out": w_expert_out, "cotangent": cotangent}


NORM_EPSILON = 1e-06
HIGHEST_PRECISION = lax.Precision.HIGHEST

@jax.custom_vjp
def low(v):
    return lax.optimization_barrier(v.astype(jnp.bfloat16)).astype(jnp.float32)

@jax.custom_vjp
def low_back(v):
    return v

def low_keep(v):
    return (low(v), None)

def low_pass(kept, grad):
    return (grad,)

def back_keep(v):
    return (v, None)

def back_low(kept, grad):
    return (low(grad),)
low.defvjp(low_keep, low_pass)
low_back.defvjp(back_keep, back_low)

def rms_scaled(values, gain_vec):
    return values * lax.rsqrt(lax.optimization_barrier(jnp.mean(values * values, axis=-1, keepdims=True)) + NORM_EPSILON) * gain_vec

def softmax_rows(scores):
    shifted = scores - lax.optimization_barrier(jnp.max(scores, axis=-1, keepdims=True))
    weights = jnp.exp(shifted)
    return weights / lax.optimization_barrier(jnp.sum(weights, axis=-1, keepdims=True))

def slot_tables(route_rows):
    row_count = route_rows.shape[0]
    onehot = (route_rows[:, :, None] == jnp.arange(EXPERTS, dtype=jnp.int32)[None, None, :]).astype(jnp.int32)
    flat_hits = onehot.reshape(2 * row_count, EXPERTS)
    before = jnp.cumsum(flat_hits, axis=0, dtype=jnp.int32) - flat_hits
    slot_index = lax.optimization_barrier(jnp.sum(before * flat_hits, axis=1, dtype=jnp.int32)).reshape(row_count, 2)
    slot_place = (route_rows * CAP + slot_index).astype(jnp.int32)
    token_ids = jnp.repeat(jnp.arange(row_count, dtype=jnp.int32), 2)
    token_of_slot = jnp.zeros((EXPERTS * CAP,), jnp.int32).at[slot_place.reshape(-1)].set(token_ids)
    return (slot_place, token_of_slot)

def attend_sequence(qkv_seq, segments, bias_vec):
    split_rows = qkv_seq.reshape(SEQ, 3, HEADS, HEAD_DIM)
    queries = split_rows[:, 0]
    key_rows = split_rows[:, 1]
    value_rows = split_rows[:, 2]
    inv_root = HEAD_DIM ** (-0.5)
    block_rows = min(512, SEQ)
    starts = jnp.arange(SEQ // block_rows, dtype=jnp.int32) * block_rows

    def one_block(offset):
        query_rows = lax.dynamic_slice_in_dim(queries, offset, block_rows, 0)
        query_pos = offset + jnp.arange(block_rows, dtype=jnp.int32)
        distance = query_pos[:, None] - jnp.arange(SEQ, dtype=jnp.int32)[None, :]
        row_segments = lax.dynamic_slice_in_dim(segments, offset, block_rows, 0)
        allowed = (distance >= 0) & (row_segments[:, None] == segments[None, :])
        bias_rows = jnp.take(bias_vec, jnp.maximum(distance, 0), axis=1)
        raw_scores = jnp.einsum('qhd,khd->hqk', query_rows, key_rows, precision=HIGHEST_PRECISION) * inv_root + bias_rows
        scores = jnp.where(allowed[None], low_back(raw_scores), -1e+30)
        return jnp.einsum('hqk,khd->qhd', low(softmax_rows(scores)), value_rows, precision=HIGHEST_PRECISION)
    mixed_heads = lax.map(jax.checkpoint(one_block), starts)
    return mixed_heads.reshape(SEQ, HEADS * HEAD_DIM)

def layer_block(token_rows, segments, route_rows, bias_vec, gain_one, qkv_weight, attn_weight, gain_two, router_weight, w_in_all, w_out_all):
    act_one = low(rms_scaled(token_rows, gain_one))
    qkv_rows = low(low_back(jnp.dot(act_one, qkv_weight, precision=HIGHEST_PRECISION)))
    seq_rows = qkv_rows.reshape(-1, SEQ, 3 * D)
    seq_segments = segments.reshape(-1, SEQ)
    heads_out = lax.map(lambda paired: attend_sequence(paired[0], paired[1], bias_vec), (seq_rows, seq_segments))
    attended = low(low_back(heads_out.reshape(-1, D)))
    residual = token_rows + low_back(jnp.dot(attended, attn_weight, precision=HIGHEST_PRECISION))
    act_two = low(rms_scaled(residual, gain_two))
    logits = low_back(jnp.dot(act_two, router_weight, precision=HIGHEST_PRECISION))
    prob_all = softmax_rows(logits)
    chosen = jnp.take_along_axis(prob_all, route_rows, axis=1)
    gate_vals = chosen / lax.optimization_barrier(jnp.sum(chosen, axis=1, keepdims=True))
    slot_place, token_of_slot = slot_tables(route_rows)
    dispatched = act_two[token_of_slot].reshape(EXPERTS, CAP, D)
    hidden = low_back(jnp.einsum('ecd,edf->ecf', dispatched, w_in_all, precision=HIGHEST_PRECISION))
    activated = low(jax.nn.gelu(hidden, approximate=True))
    expert_rows = low_back(jnp.einsum('ecf,efd->ecd', activated, w_out_all, precision=HIGHEST_PRECISION)).reshape(EXPERTS * CAP, D)
    picked = expert_rows[slot_place]
    return residual + lax.optimization_barrier(jnp.sum(gate_vals[:, :, None] * picked, axis=1))

def reference(tokens, segment_ids, routes, buckets, norm1_gain, w_qkv, w_attn_out, bias_table, norm2_gain, router, w_in, w_expert_out, cotangent):
    floats = tuple((item.astype(jnp.float32) for item in (tokens, norm1_gain, w_qkv, w_attn_out, bias_table, norm2_gain, router, w_in, w_expert_out)))

    def whole_layer(token_rows, gain_one, qkv_weight, attn_weight, bias_full, gain_two, router_weight, w_in_all, w_out_all):
        bias_vec = jnp.take(bias_full, buckets, axis=0).T
        block_step = jax.checkpoint(lambda inputs: layer_block(inputs[0], inputs[1], inputs[2], bias_vec, gain_one, qkv_weight, attn_weight, gain_two, router_weight, w_in_all, w_out_all))
        block_outs = lax.map(block_step, (token_rows.reshape(-1, TOK_DEV, D), segment_ids.reshape(-1, TOK_DEV), routes.reshape(-1, TOK_DEV, 2)))
        return block_outs.reshape(-1, D)
    mixed_out, pullback = jax.vjp(whole_layer, *floats)
    gradients = pullback(cotangent.astype(jnp.float32))
    return (mixed_out.astype(jnp.bfloat16), gradients[0].astype(jnp.bfloat16), gradients[1], gradients[2], gradients[3], gradients[4], gradients[5], gradients[6], gradients[7], gradients[8])
```

```python
import functools

import jax
import jax.numpy as jnp
from jax import lax
from jax.experimental import pallas as pl
from jax.experimental.pallas import tpu as pltpu
from jax.sharding import PartitionSpec as P

D = 768
HEADS = 12
HEAD_DIM = 64
FF = 3072
EXPERTS = 4
BUCKETS = 32
SEQ = 1024
CAP = 640
BLOCK = 256
REACH = 768
NORM_EPSILON = 1e-06
HIGHEST = lax.Precision.HIGHEST
NEG = -1e30
F32 = jnp.float32
BF16 = jnp.bfloat16
MIB = 1024 * 1024
GELU_ROOT = 0.7978845608028654
GELU_CUBE = 0.044715


def norm_forward(values, gain_vec):
    inv_rms = lax.rsqrt(jnp.mean(values * values, axis=-1, keepdims=True) + NORM_EPSILON)
    unit_rows = values * inv_rms
    return unit_rows, inv_rms, unit_rows * gain_vec


def norm_backward(grad_norm, unit_rows, inv_rms, gain_vec):
    grad_unit = grad_norm * gain_vec
    grad_gain = jnp.sum(grad_norm * unit_rows, axis=0)
    grad_input = inv_rms * (
        grad_unit - unit_rows * jnp.mean(grad_unit * unit_rows, axis=-1, keepdims=True)
    )
    return grad_input, grad_gain


def key_span(block):
    low = max(0, (block + 1) * BLOCK - REACH)
    return low, (block + 1) * BLOCK - low


def fill_mask(seg_col_ref, seg_row_ref, mask_ref):
    for block in range(SEQ // BLOCK):
        low, width = key_span(block)
        same = (
            seg_col_ref[low : low + width, :]
            == seg_row_ref[:, block * BLOCK : (block + 1) * BLOCK]
        )
        mask_ref[block, REACH - width :, :] = jnp.where(same, 0.0, NEG)


def fill_bias(line_ref, bias_ref):
    for head in range(2):
        for part in range(3):
            rows = line_ref[0, 3 * head + part : 3 * head + part + 1, :]
            count = 1
            while count < BLOCK:
                rows = jnp.concatenate([rows, pltpu.roll(rows, count, 1)], axis=0)
                count *= 2
            bias_ref[head, part * BLOCK : (part + 1) * BLOCK, :] = rows[:, :BLOCK]


def diagonal_sums(square):
    rows = jnp.concatenate([square, jnp.zeros_like(square)], axis=1)
    count = BLOCK
    while count > 1:
        count //= 2
        rows = rows[:count] + pltpu.roll(rows[count:], 2 * BLOCK - count, 1)
    return rows


def head_lanes(head, rows):
    lane = lax.broadcasted_iota(jnp.int32, rows.shape, 1)
    return jnp.where(lane // HEAD_DIM == head, rows, jnp.zeros_like(rows))


def dot_nt(left, right):
    return lax.dot_general(left, right, (((1,), (1,)), ((), ())), preferred_element_type=F32)


def dot_nn(left, right):
    return jnp.dot(left, right, preferred_element_type=F32)


def attention_kernel(
    q_ref, k_ref, v_ref, seg_col_ref, seg_row_ref, line_ref, out_ref, total_ref, mask_ref, bias_ref
):
    @pl.when(pl.program_id(0) == 0)
    def _():
        fill_mask(seg_col_ref, seg_row_ref, mask_ref)

    fill_bias(line_ref, bias_ref)
    values_t = v_ref[...].T
    for block in range(SEQ // BLOCK):
        low, width = key_span(block)
        here = slice(block * BLOCK, (block + 1) * BLOCK)
        queries = q_ref[here, :] * jnp.asarray(HEAD_DIM**-0.5, BF16)
        parts = []
        for head in range(2):
            scores = dot_nt(k_ref[low : low + width, :], head_lanes(head, queries))
            scores = scores + bias_ref[head, REACH - width :, :] + mask_ref[block, REACH - width :, :]
            top = jnp.max(scores, axis=0, keepdims=True)
            weights = jnp.exp(scores - top)
            denom = jnp.sum(weights, axis=0, keepdims=True)
            mixed = dot_nn(values_t[:, low : low + width], weights.astype(BF16))
            parts.append(mixed[head * HEAD_DIM : (head + 1) * HEAD_DIM, :] / denom)
            total_ref[0, head : head + 1, here] = top + jnp.log(denom)
        out_ref[here, :] = jnp.concatenate(parts, axis=0).T.astype(BF16)


def attention_back_kernel(
    q_ref, k_ref, v_ref, out_ref, grad_ref, total_ref, seg_col_ref, seg_row_ref, line_ref,
    dqkv_ref, dline_ref, mask_ref, bias_ref, dbias_ref, dk_ref, dv_ref,
):
    @pl.when(pl.program_id(0) == 0)
    def _():
        fill_mask(seg_col_ref, seg_row_ref, mask_ref)

    fill_bias(line_ref, bias_ref)
    keys_t = k_ref[...].T
    dk_ref[...] = jnp.zeros_like(dk_ref)
    dv_ref[...] = jnp.zeros_like(dv_ref)
    dbias_ref[...] = jnp.zeros_like(dbias_ref)
    scale = HEAD_DIM**-0.5
    for block in range(SEQ // BLOCK):
        low, width = key_span(block)
        here = slice(block * BLOCK, (block + 1) * BLOCK)
        span = slice(low, low + width)
        queries = q_ref[here, :] * jnp.asarray(scale, BF16)
        grads = grad_ref[here, :]
        inner = (grads.astype(F32) * out_ref[here, :].astype(F32)).T
        parts = []
        for head in range(2):
            rows = slice(head * HEAD_DIM, (head + 1) * HEAD_DIM)
            query_head = head_lanes(head, queries)
            grad_head = head_lanes(head, grads)
            scores = dot_nt(k_ref[span, :], query_head)
            scores = scores + bias_ref[head, REACH - width :, :] + mask_ref[block, REACH - width :, :]
            probs = jnp.exp(scores - total_ref[0, head : head + 1, here])
            grad_probs = dot_nt(v_ref[span, :], grad_head)
            delta = jnp.sum(inner[rows, :], axis=0, keepdims=True)
            grad_scores = probs * (grad_probs - delta)
            dbias_ref[head, REACH - width :, :] += grad_scores
            low_scores = grad_scores.astype(BF16)
            dv_ref[span, :] += dot_nn(probs.astype(BF16), grad_head)
            dk_ref[span, :] += dot_nn(low_scores, query_head)
            parts.append(dot_nn(keys_t[:, span], low_scores)[rows, :])
        dqkv_ref[0, here, :] = (jnp.concatenate(parts, axis=0).T * scale).astype(BF16)
    dqkv_ref[1, :, :] = dk_ref[...].astype(BF16)
    dqkv_ref[2, :, :] = dv_ref[...].astype(BF16)
    for head in range(2):
        for part in range(3):
            sums = diagonal_sums(dbias_ref[head, part * BLOCK : (part + 1) * BLOCK, :])
            dline_ref[0, 3 * head + part : 3 * head + part + 1, :] = sums
    dline_ref[0, 6:8, :] = jnp.zeros((2, 2 * BLOCK), F32)


def pair_spec(offset):
    return pl.BlockSpec((SEQ, 2 * HEAD_DIM), lambda pair: (0, pair + offset))


PAIRS = HEADS // 2
SEG_SPECS = [
    pl.BlockSpec((SEQ, 1), lambda pair: (0, 0)),
    pl.BlockSpec((1, SEQ), lambda pair: (0, 0)),
    pl.BlockSpec((1, 8, 2 * BLOCK), lambda pair: (pair, 0, 0)),
]
TOTAL_SPEC = pl.BlockSpec((1, 8, SEQ), lambda pair: (pair, 0, 0))
PAIR_SCRATCH = [
    pltpu.VMEM((SEQ // BLOCK, REACH, BLOCK), F32),
    pltpu.VMEM((2, REACH, BLOCK), F32),
]


def attend_forward(qkv_rows, seg_col, seg_row, lines):
    return pl.pallas_call(
        attention_kernel,
        grid=(PAIRS,),
        in_specs=[pair_spec(0), pair_spec(PAIRS), pair_spec(2 * PAIRS)] + SEG_SPECS,
        out_specs=[pair_spec(0), TOTAL_SPEC],
        out_shape=[
            jax.ShapeDtypeStruct((SEQ, D), BF16),
            jax.ShapeDtypeStruct((PAIRS, 8, SEQ), F32),
        ],
        scratch_shapes=PAIR_SCRATCH,
        compiler_params=pltpu.CompilerParams(vmem_limit_bytes=48 * MIB),
        cost_estimate=pl.CostEstimate(
            flops=4 * SEQ * SEQ * D, bytes_accessed=8 * SEQ * D, transcendentals=0
        ),
        name="attend_forward",
    )(qkv_rows, qkv_rows, qkv_rows, seg_col, seg_row, lines)


def attend_backward(qkv_rows, attended, grad_attended, totals, seg_col, seg_row, lines):
    return pl.pallas_call(
        attention_back_kernel,
        grid=(PAIRS,),
        in_specs=[
            pair_spec(0), pair_spec(PAIRS), pair_spec(2 * PAIRS), pair_spec(0), pair_spec(0), TOTAL_SPEC,
        ] + SEG_SPECS,
        out_specs=[
            pl.BlockSpec((3, SEQ, 2 * HEAD_DIM), lambda pair: (0, 0, pair)),
            pl.BlockSpec((1, 8, 2 * BLOCK), lambda pair: (pair, 0, 0)),
        ],
        out_shape=[
            jax.ShapeDtypeStruct((3, SEQ, D), BF16),
            jax.ShapeDtypeStruct((PAIRS, 8, 2 * BLOCK), F32),
        ],
        scratch_shapes=PAIR_SCRATCH + [
            pltpu.VMEM((2, REACH, BLOCK), F32),
            pltpu.VMEM((SEQ, 2 * HEAD_DIM), F32),
            pltpu.VMEM((SEQ, 2 * HEAD_DIM), F32),
        ],
        compiler_params=pltpu.CompilerParams(vmem_limit_bytes=48 * MIB),
        cost_estimate=pl.CostEstimate(
            flops=10 * SEQ * SEQ * D, bytes_accessed=16 * SEQ * D, transcendentals=0
        ),
        name="attend_backward",
    )(qkv_rows, qkv_rows, qkv_rows, attended, grad_attended, totals, seg_col, seg_row, lines)


def bias_lines(bias_vec):
    reach = jnp.concatenate([jnp.full((HEADS, BLOCK), NEG, F32), bias_vec], axis=1)
    parts = []
    for part in range(3):
        middle = REACH - part * BLOCK
        parts.append(
            jnp.concatenate([reach[:, middle : middle + BLOCK], reach[:, middle - BLOCK : middle]], axis=1)
        )
    lines = jnp.stack(parts, axis=1).reshape(PAIRS, 6, 2 * BLOCK)
    return jnp.concatenate([lines, jnp.zeros((PAIRS, 2, 2 * BLOCK), F32)], axis=1)


def bias_line_grads(grad_lines):
    parts = grad_lines[:, :6].reshape(HEADS, 3, 2 * BLOCK)
    total = jnp.zeros((HEADS, SEQ + BLOCK), F32)
    for part in range(3):
        middle = REACH - part * BLOCK
        line = jnp.concatenate([parts[:, part, BLOCK:], parts[:, part, :BLOCK]], axis=1)
        total = total + jnp.pad(line, ((0, 0), (middle - BLOCK, SEQ - middle)))
    return total[:, BLOCK:]


FF_BLOCK = 512


def expert_kernel(
    rows_ref, grad_ref, gate_ref, w_in_ref, w_out_ref,
    act_ref, dhid_ref, dout_ref, out_ref, drow_ref, dgate_ref, out_acc, drow_acc,
):
    gates = gate_ref[...]
    dout_ref[...] = (gates * grad_ref[...].astype(F32)).astype(BF16)
    out_acc[...] = jnp.zeros_like(out_acc)
    drow_acc[...] = jnp.zeros_like(drow_acc)

    def step(index, carry):
        cols = pl.ds(pl.multiple_of(index * FF_BLOCK, FF_BLOCK), FF_BLOCK)
        w_in = w_in_ref[:, cols]
        w_out = w_out_ref[cols, :]
        hidden = dot_nn(rows_ref[...], w_in)
        grad_act = dot_nt(dout_ref[...], w_out)
        square = hidden * hidden
        bend = jnp.tanh(hidden * (GELU_ROOT + (GELU_ROOT * GELU_CUBE) * square))
        half = 0.5 + 0.5 * bend
        act = (hidden * half).astype(BF16)
        slope = half + 0.5 * hidden * (1.0 - bend * bend) * (
            GELU_ROOT + (3.0 * GELU_ROOT * GELU_CUBE) * square
        )
        dhid = (grad_act * slope).astype(BF16)
        act_ref[:, cols] = act
        dhid_ref[:, cols] = dhid
        out_acc[...] += dot_nn(act, w_out)
        drow_acc[...] += dot_nt(dhid, w_in)
        return carry

    lax.fori_loop(0, FF // FF_BLOCK, step, 0)
    outs = out_acc[...]
    out_ref[...] = (gates * outs).astype(BF16)
    drow_ref[...] = drow_acc[...].astype(BF16)
    dgate_ref[...] = jnp.sum(grad_ref[...].astype(F32) * outs, axis=1, keepdims=True)


def run_expert(rows, grads, gates, w_in, w_out):
    count = rows.shape[0] // CAP
    row_spec = pl.BlockSpec((CAP, D), lambda part: (part, 0))
    wide_spec = pl.BlockSpec((CAP, FF), lambda part: (part, 0))
    gate_spec = pl.BlockSpec((CAP, 1), lambda part: (part, 0))
    once = pl.Buffered(1)
    narrow = jax.ShapeDtypeStruct((count * CAP, D), BF16)
    wide = jax.ShapeDtypeStruct((count * CAP, FF), BF16)
    return pl.pallas_call(
        expert_kernel,
        grid=(count,),
        in_specs=[
            row_spec,
            row_spec,
            gate_spec,
            pl.BlockSpec((D, FF), lambda part: (0, 0), pipeline_mode=once),
            pl.BlockSpec((FF, D), lambda part: (0, 0), pipeline_mode=once),
        ],
        out_specs=[wide_spec, wide_spec, row_spec, row_spec, row_spec, gate_spec],
        out_shape=[wide, wide, narrow, narrow, narrow, jax.ShapeDtypeStruct((count * CAP, 1), F32)],
        scratch_shapes=[pltpu.VMEM((CAP, D), F32), pltpu.VMEM((CAP, D), F32)],
        compiler_params=pltpu.CompilerParams(vmem_limit_bytes=56 * MIB),
        cost_estimate=pl.CostEstimate(
            flops=8 * count * CAP * D * FF, bytes_accessed=4 * D * FF + 4 * count * CAP * FF, transcendentals=0
        ),
        name="run_expert",
    )(rows, grads, gates, w_in, w_out)


def split_three(values):
    first = values.astype(BF16)
    rest = values - first.astype(F32)
    second = rest.astype(BF16)
    third = (rest - second.astype(F32)).astype(BF16)
    return jnp.stack([first, second, third], axis=-1)


def body(
    dp_size, tokens, segment_ids, routes, buckets, norm1_gain, w_qkv, w_attn_out, bias_table,
    norm2_gain, router, w_in, w_expert_out, cotangent,
):
    shard_rows = w_qkv.shape[0]
    table_rows = bias_table.shape[0]
    me = lax.axis_index("dp") % EXPERTS

    def swap(value, relation):
        if relation == 0:
            return value
        return lax.ppermute(value, "dp", [(i, i ^ relation) for i in range(dp_size)])

    def spread(value):
        across = swap(value, 2)
        return [value, swap(value, 1), across, swap(across, 1)]

    table_col = jnp.pad(bias_table.reshape(-1), (0, shard_rows - table_rows * HEADS))
    small = jnp.concatenate(
        [norm1_gain[:, None], norm2_gain[:, None], router, table_col[:, None]], axis=1
    )
    packed = jnp.concatenate([w_qkv, w_attn_out, jnp.pad(small, ((0, 0), (0, 121)))], axis=1)
    packed = lax.all_gather(packed, "shard", axis=0, tiled=True)
    qkv_weight = packed[:, : 3 * D]
    attn_weight = packed[:, 3 * D : 4 * D]
    gain_one = packed[:, 4 * D].astype(F32)
    gain_two = packed[:, 4 * D + 1].astype(F32)
    router_weight = packed[:, 4 * D + 2 : 4 * D + 6]
    bias_full = packed[:, 4 * D + 6].reshape(-1, shard_rows)[:, : table_rows * HEADS].reshape(BUCKETS, HEADS)

    my_in = lax.dynamic_index_in_dim(w_in, me, 0, keepdims=False)
    my_out = lax.dynamic_index_in_dim(w_expert_out, me, 0, keepdims=False)
    full_in = lax.all_gather(my_in, "shard", axis=0, tiled=True)
    full_out = lax.all_gather(my_out, "shard", axis=0, tiled=True)

    cot_parts = spread(cotangent)

    expert_ids = jnp.arange(EXPERTS, dtype=jnp.int32)
    hits = (
        (routes[:, 0][None, :] == expert_ids[:, None]) | (routes[:, 1][None, :] == expert_ids[:, None])
    ).astype(F32)
    token_ids = jnp.arange(SEQ, dtype=jnp.int32)
    before = (token_ids[:, None] < token_ids[None, :]).astype(BF16)
    places = jnp.dot(hits.astype(BF16), before, preferred_element_type=F32)
    keys = jnp.where(hits > 0, places, -1.0)
    relation_ids = me ^ expert_ids

    def related(rows):
        return [lax.dynamic_index_in_dim(rows, relation_ids[x], 0, keepdims=False) for x in range(EXPERTS)]

    slot_ids = jnp.arange(CAP, dtype=F32)

    def pick_matrix(key_row):
        return (key_row[None, :] == slot_ids[:, None]).astype(BF16)

    my_keys = related(keys)
    their_picks = [pick_matrix(swap(my_keys[x], x)) for x in range(EXPERTS)]
    my_picks = jnp.concatenate([pick_matrix(my_keys[x]) for x in range(EXPERTS)], axis=0)
    grad_slots = [
        jnp.dot(their_picks[x], cot_parts[x], preferred_element_type=F32).astype(BF16) for x in range(EXPERTS)
    ]

    bucket_hits = (jnp.arange(BUCKETS, dtype=jnp.int32)[:, None] == buckets[None, :]).astype(BF16)
    bias_vec = lax.dot_general(bias_full, bucket_hits, (((0,), (0,)), ((), ())), preferred_element_type=F32)
    lines = bias_lines(bias_vec)
    seg_col, seg_row = segment_ids[:, None], segment_ids[None, :]

    token_rows = tokens.astype(F32)
    unit_one, inv_one, normed_one = norm_forward(token_rows, gain_one)
    act_one = normed_one.astype(BF16)
    qkv_rows = jnp.dot(act_one, qkv_weight, preferred_element_type=F32).astype(BF16)
    attended, totals = attend_forward(qkv_rows, seg_col, seg_row, lines)
    residual = token_rows + jnp.dot(attended, attn_weight, preferred_element_type=F32)
    unit_two, inv_two, normed_two = norm_forward(residual, gain_two)
    act_two = normed_two.astype(BF16)
    act_parts = spread(act_two)

    logits = lax.dot_general(router_weight, act_two, (((0,), (1,)), ((), ())), preferred_element_type=F32)
    shifted = jnp.exp(logits - jnp.max(logits, axis=0, keepdims=True))
    prob_all = shifted / jnp.sum(shifted, axis=0, keepdims=True)
    chosen_sum = jnp.sum(hits * prob_all, axis=0, keepdims=True)
    gates = hits * prob_all / chosen_sum
    my_gates = related(gates)
    their_gates = [swap(my_gates[x], x) for x in range(EXPERTS)]

    def dispatch(relations):
        rows = jnp.concatenate(
            [jnp.dot(their_picks[x], act_parts[x], preferred_element_type=F32).astype(BF16) for x in relations], axis=0
        )
        gate_col = jnp.concatenate(
            [
                jnp.sum(
                    jnp.dot(their_picks[x], split_three(their_gates[x]), preferred_element_type=F32),
                    axis=1,
                    keepdims=True,
                )
                for x in relations
            ],
            axis=0,
        )
        return rows, gate_col

    halves = []
    for relations in ((0, 1), (2, 3)):
        rows, gate_col = dispatch(relations)
        grads = jnp.concatenate([grad_slots[x] for x in relations], axis=0)
        halves.append((rows,) + tuple(run_expert(rows, grads, gate_col, full_in, full_out)))

    def back_to_tokens(picks, dgate_rows):
        parts = split_three(dgate_rows[:, 0])
        return jnp.sum(
            lax.dot_general(parts, picks, (((0,), (0,)), ((), ())), preferred_element_type=F32), axis=0
        )

    out_parts, drow_parts, dgate_parts = [], [], []
    for half, relations in zip(halves, ((0, 1), (2, 3))):
        _, _, _, _, outs, drows, dgates = half
        for index, x in enumerate(relations):
            part = slice(index * CAP, (index + 1) * CAP)
            drow_parts.append(swap(drows[part], x))
            out_parts.append(swap(outs[part], x))
            dgate_parts.append(swap(back_to_tokens(their_picks[x], dgates[part]), x))

    def weight_grad(left, right):
        total = lax.dot_general(left[0], right[0], (((0,), (0,)), ((), ())), preferred_element_type=F32)
        total += lax.dot_general(left[1], right[1], (((0,), (0,)), ((), ())), preferred_element_type=F32)
        return total.astype(BF16)

    grad_in = weight_grad([h[0] for h in halves], [h[2] for h in halves])
    grad_out = weight_grad([h[1] for h in halves], [h[3] for h in halves])
    grad_in = lax.psum_scatter(grad_in, "shard", scatter_dimension=0, tiled=True)
    grad_out = lax.psum_scatter(grad_out, "shard", scatter_dimension=0, tiled=True)

    def over_groups(value):
        total = value.astype(F32)
        for group in range(1, dp_size // EXPERTS):
            moved = lax.ppermute(value, "dp", [(i, (i + EXPERTS * group) % dp_size) for i in range(dp_size)])
            total = total + moved.astype(F32)
        return total.astype(BF16)

    def place(value):
        parts = spread(over_groups(value))
        out = jnp.zeros((EXPERTS,) + value.shape, F32)
        for x in range(EXPERTS):
            out = lax.dynamic_update_index_in_dim(out, parts[x].astype(F32), relation_ids[x], 0)
        return out

    grad_w_in = place(grad_in)
    grad_w_out = place(grad_out)

    def collect(parts):
        stacked = jnp.concatenate(parts, axis=0)
        return lax.dot_general(my_picks, stacked, (((0,), (0,)), ((), ())), preferred_element_type=F32)

    mixed_out = (residual + collect(out_parts)).astype(BF16)
    grad_act_two = collect(drow_parts)
    grad_gates = jnp.stack(related(jnp.stack(dgate_parts, axis=0)), axis=0)
    weighted = jnp.sum(grad_gates * gates, axis=0, keepdims=True)
    grad_prob = hits * (grad_gates - weighted) / chosen_sum
    grad_logits = (prob_all * (grad_prob - jnp.sum(prob_all * grad_prob, axis=0, keepdims=True))).astype(BF16)
    grad_router = lax.dot_general(act_two, grad_logits, (((0,), (1,)), ((), ())), preferred_element_type=F32)
    grad_act_two = grad_act_two + lax.dot_general(
        grad_logits, router_weight, (((0,), (1,)), ((), ())), preferred_element_type=F32
    )
    grad_norm_two, grad_gain_two = norm_backward(grad_act_two, unit_two, inv_two, gain_two)
    grad_residual = cotangent.astype(F32) + grad_norm_two
    grad_branch = grad_residual.astype(BF16)
    grad_attn_weight = lax.dot_general(
        attended, grad_branch, (((0,), (0,)), ((), ())), preferred_element_type=F32
    )
    grad_attended = dot_nt(grad_branch, attn_weight).astype(BF16)
    grad_split, grad_lines = attend_backward(
        qkv_rows, attended, grad_attended, totals, seg_col, seg_row, lines
    )
    grad_act_one = sum(dot_nt(grad_split[i], qkv_weight[:, i * D : (i + 1) * D]) for i in range(3))
    grad_qkv_weight = [
        lax.dot_general(act_one, grad_split[i], (((0,), (0,)), ((), ())), preferred_element_type=F32)
        for i in range(3)
    ]
    grad_norm_one, grad_gain_one = norm_backward(grad_act_one, unit_one, inv_one, gain_one)
    grad_tokens = (grad_residual + grad_norm_one).astype(BF16)
    grad_table = lax.dot_general(
        bucket_hits.astype(F32), bias_line_grads(grad_lines), (((1,), (1,)), ((), ())), precision=HIGHEST
    )
    shards = D // shard_rows
    table_sums = jnp.pad(
        grad_table.reshape(shards, table_rows * HEADS), ((0, 0), (0, shard_rows - table_rows * HEADS))
    ).reshape(D, 1)
    small = jnp.concatenate([grad_gain_one[:, None], grad_gain_two[:, None], grad_router, table_sums], axis=1)
    packed = jnp.concatenate(
        [g.astype(BF16) for g in grad_qkv_weight]
        + [grad_attn_weight.astype(BF16), jnp.pad(small, ((0, 0), (0, 121))).astype(BF16)],
        axis=1,
    )
    packed = lax.psum_scatter(packed, "shard", scatter_dimension=0, tiled=True).astype(F32)
    packed = lax.psum(packed, "dp")
    return (
        mixed_out,
        grad_tokens,
        packed[:, 4 * D],
        packed[:, : 3 * D],
        packed[:, 3 * D : 4 * D],
        packed[:, 4 * D + 6][: table_rows * HEADS].reshape(table_rows, HEADS),
        packed[:, 4 * D + 1],
        packed[:, 4 * D + 2 : 4 * D + 6],
        grad_w_in,
        grad_w_out,
    )


def solution(mesh):
    return jax.shard_map(
        functools.partial(body, mesh.shape["dp"]),
        mesh=mesh,
        in_specs=(
            P(("dp", "shard"), None),
            P(("dp", "shard")),
            P(("dp", "shard"), None),
            P(),
            P("shard"),
            P("shard", None),
            P("shard", None),
            P("shard", None),
            P("shard"),
            P("shard", None),
            P(None, "shard", None),
            P(None, "shard", None),
            P(("dp", "shard"), None),
        ),
        out_specs=(
            P(("dp", "shard"), None),
            P(("dp", "shard"), None),
            P("shard"),
            P("shard", None),
            P("shard", None),
            P("shard", None),
            P("shard"),
            P("shard", None),
            P(None, "shard", None),
            P(None, "shard", None),
        ),
        check_vma=False,
    )
```

```python
import functools

import jax
import jax.numpy as jnp
from jax import lax
from jax.experimental import pallas as pl
from jax.experimental.pallas import tpu as pltpu
from jax.sharding import PartitionSpec as P

D = 768
HEADS = 12
HEAD_DIM = 64
FF = 3072
EXPERTS = 4
BUCKETS = 32
SEQ = 1024
CAP = 640
DEEP = 4
BLOCK = 256
REACH = 768
NORM_EPSILON = 1e-06
HIGHEST = lax.Precision.HIGHEST
NEG = -1e30
COST_CUT = 256
F32 = jnp.float32
BF16 = jnp.bfloat16
MIB = 1024 * 1024
GELU_ROOT = 0.7978845608028654
GELU_CUBE = 0.044715


def norm_forward(values, gain_vec):
    inv_rms = lax.rsqrt(jnp.mean(values * values, axis=-1, keepdims=True) + NORM_EPSILON)
    unit_rows = values * inv_rms
    return unit_rows, inv_rms, unit_rows * gain_vec


def cost(flops, moved):
    return pl.CostEstimate(flops=flops // COST_CUT, bytes_accessed=moved // COST_CUT, transcendentals=0)


def key_span(block):
    low = max(0, (block + 1) * BLOCK - REACH)
    return low, (block + 1) * BLOCK - low


def fill_mask(seg_col_ref, seg_row_ref, mask_ref):
    for block in range(SEQ // BLOCK):
        low, width = key_span(block)
        same = (
            seg_col_ref[low : low + width, :]
            == seg_row_ref[:, block * BLOCK : (block + 1) * BLOCK]
        )
        mask_ref[block, REACH - width :, :] = jnp.where(same, 0.0, NEG)


def fill_bias(line_ref, bias_ref):
    for head in range(2):
        for part in range(3):
            rows = line_ref[0, 3 * head + part : 3 * head + part + 1, :]
            count = 1
            while count < BLOCK:
                rows = jnp.concatenate([rows, pltpu.roll(rows, count, 1)], axis=0)
                count *= 2
            bias_ref[head, part * BLOCK : (part + 1) * BLOCK, :] = rows[:, :BLOCK]


def diagonal_sums(square):
    rows = jnp.concatenate([square, jnp.zeros_like(square)], axis=1)
    count = BLOCK
    while count > 1:
        count //= 2
        rows = rows[:count] + pltpu.roll(rows[count:], 2 * BLOCK - count, 1)
    return rows


def head_lanes(head, rows):
    lane = lax.broadcasted_iota(jnp.int32, rows.shape, 1)
    return jnp.where(lane // HEAD_DIM == head, rows, jnp.zeros_like(rows))


def dot_nt(left, right):
    return lax.dot_general(left, right, (((1,), (1,)), ((), ())), preferred_element_type=F32)


def dot_nn(left, right):
    return jnp.dot(left, right, preferred_element_type=F32)


def attention_kernel(
    q_ref, k_ref, v_ref, seg_col_ref, seg_row_ref, line_ref, out_ref, total_ref, mask_ref, bias_ref
):
    @pl.when(pl.program_id(0) == 0)
    def _():
        fill_mask(seg_col_ref, seg_row_ref, mask_ref)

    fill_bias(line_ref, bias_ref)
    values_t = v_ref[...].T
    for block in range(SEQ // BLOCK):
        low, width = key_span(block)
        here = slice(block * BLOCK, (block + 1) * BLOCK)
        queries = q_ref[here, :] * jnp.asarray(HEAD_DIM**-0.5, BF16)
        parts = []
        for head in range(2):
            scores = dot_nt(k_ref[low : low + width, :], head_lanes(head, queries))
            scores = scores + bias_ref[head, REACH - width :, :] + mask_ref[block, REACH - width :, :]
            top = jnp.max(scores, axis=0, keepdims=True)
            weights = jnp.exp(scores - top)
            denom = jnp.sum(weights, axis=0, keepdims=True)
            mixed = dot_nn(values_t[:, low : low + width], weights.astype(BF16))
            parts.append(mixed[head * HEAD_DIM : (head + 1) * HEAD_DIM, :] / denom)
            total_ref[0, head : head + 1, here] = top + jnp.log(denom)
        out_ref[here, :] = jnp.concatenate(parts, axis=0).T.astype(BF16)


def attention_back_kernel(
    q_ref, k_ref, v_ref, out_ref, grad_ref, total_ref, seg_col_ref, seg_row_ref, line_ref,
    dqkv_ref, dline_ref, mask_ref, bias_ref, dbias_ref, dk_ref, dv_ref,
):
    @pl.when(pl.program_id(0) == 0)
    def _():
        fill_mask(seg_col_ref, seg_row_ref, mask_ref)

    fill_bias(line_ref, bias_ref)
    keys_t = k_ref[...].T
    dk_ref[...] = jnp.zeros_like(dk_ref)
    dv_ref[...] = jnp.zeros_like(dv_ref)
    dbias_ref[...] = jnp.zeros_like(dbias_ref)
    scale = HEAD_DIM**-0.5
    for block in range(SEQ // BLOCK):
        low, width = key_span(block)
        here = slice(block * BLOCK, (block + 1) * BLOCK)
        span = slice(low, low + width)
        queries = q_ref[here, :] * jnp.asarray(scale, BF16)
        grads = grad_ref[here, :]
        inner = (grads.astype(F32) * out_ref[here, :].astype(F32)).T
        parts = []
        for head in range(2):
            rows = slice(head * HEAD_DIM, (head + 1) * HEAD_DIM)
            query_head = head_lanes(head, queries)
            grad_head = head_lanes(head, grads)
            scores = dot_nt(k_ref[span, :], query_head)
            scores = scores + bias_ref[head, REACH - width :, :] + mask_ref[block, REACH - width :, :]
            probs = jnp.exp(scores - total_ref[0, head : head + 1, here])
            grad_probs = dot_nt(v_ref[span, :], grad_head)
            delta = jnp.sum(inner[rows, :], axis=0, keepdims=True)
            grad_scores = probs * (grad_probs - delta)
            dbias_ref[head, REACH - width :, :] += grad_scores
            low_scores = grad_scores.astype(BF16)
            dv_ref[span, :] += dot_nn(probs.astype(BF16), grad_head)
            dk_ref[span, :] += dot_nn(low_scores, query_head)
            parts.append(dot_nn(keys_t[:, span], low_scores)[rows, :])
        dqkv_ref[0, here, :] = (jnp.concatenate(parts, axis=0).T * scale).astype(BF16)
    dqkv_ref[1, :, :] = dk_ref[...].astype(BF16)
    dqkv_ref[2, :, :] = dv_ref[...].astype(BF16)
    for head in range(2):
        for part in range(3):
            sums = diagonal_sums(dbias_ref[head, part * BLOCK : (part + 1) * BLOCK, :])
            dline_ref[0, 3 * head + part : 3 * head + part + 1, :] = sums
    dline_ref[0, 6:8, :] = jnp.zeros((2, 2 * BLOCK), F32)


def pair_spec(offset):
    return pl.BlockSpec((SEQ, 2 * HEAD_DIM), lambda pair: (0, pair + offset))


PAIRS = HEADS // 2
SEG_SPECS = [
    pl.BlockSpec((SEQ, 1), lambda pair: (0, 0)),
    pl.BlockSpec((1, SEQ), lambda pair: (0, 0)),
    pl.BlockSpec((1, 8, 2 * BLOCK), lambda pair: (pair, 0, 0)),
]
TOTAL_SPEC = pl.BlockSpec((1, 8, SEQ), lambda pair: (pair, 0, 0))
PAIR_SCRATCH = [
    pltpu.VMEM((SEQ // BLOCK, REACH, BLOCK), F32),
    pltpu.VMEM((2, REACH, BLOCK), F32),
]


def attend_forward(qkv_rows, seg_col, seg_row, lines):
    return pl.pallas_call(
        attention_kernel,
        grid=(PAIRS,),
        in_specs=[pair_spec(0), pair_spec(PAIRS), pair_spec(2 * PAIRS)] + SEG_SPECS,
        out_specs=[pair_spec(0), TOTAL_SPEC],
        out_shape=[
            jax.ShapeDtypeStruct((SEQ, D), BF16),
            jax.ShapeDtypeStruct((PAIRS, 8, SEQ), F32),
        ],
        scratch_shapes=PAIR_SCRATCH,
        compiler_params=pltpu.CompilerParams(vmem_limit_bytes=48 * MIB),
        cost_estimate=cost(4 * SEQ * SEQ * D, 8 * SEQ * D),
        name="attend_forward",
    )(qkv_rows, qkv_rows, qkv_rows, seg_col, seg_row, lines)


def attend_backward(qkv_rows, attended, grad_attended, totals, seg_col, seg_row, lines):
    return pl.pallas_call(
        attention_back_kernel,
        grid=(PAIRS,),
        in_specs=[
            pair_spec(0), pair_spec(PAIRS), pair_spec(2 * PAIRS), pair_spec(0), pair_spec(0), TOTAL_SPEC,
        ] + SEG_SPECS,
        out_specs=[
            pl.BlockSpec((3, SEQ, 2 * HEAD_DIM), lambda pair: (0, 0, pair)),
            pl.BlockSpec((1, 8, 2 * BLOCK), lambda pair: (pair, 0, 0)),
        ],
        out_shape=[
            jax.ShapeDtypeStruct((3, SEQ, D), BF16),
            jax.ShapeDtypeStruct((PAIRS, 8, 2 * BLOCK), F32),
        ],
        scratch_shapes=PAIR_SCRATCH + [
            pltpu.VMEM((2, REACH, BLOCK), F32),
            pltpu.VMEM((SEQ, 2 * HEAD_DIM), F32),
            pltpu.VMEM((SEQ, 2 * HEAD_DIM), F32),
        ],
        compiler_params=pltpu.CompilerParams(vmem_limit_bytes=48 * MIB),
        cost_estimate=cost(10 * SEQ * SEQ * D, 16 * SEQ * D),
        name="attend_backward",
    )(qkv_rows, qkv_rows, qkv_rows, attended, grad_attended, totals, seg_col, seg_row, lines)


def bias_lines(bias_vec):
    reach = jnp.concatenate([jnp.full((HEADS, BLOCK), NEG, F32), bias_vec], axis=1)
    parts = []
    for part in range(3):
        middle = REACH - part * BLOCK
        parts.append(
            jnp.concatenate([reach[:, middle : middle + BLOCK], reach[:, middle - BLOCK : middle]], axis=1)
        )
    lines = jnp.stack(parts, axis=1).reshape(PAIRS, 6, 2 * BLOCK)
    return jnp.concatenate([lines, jnp.zeros((PAIRS, 2, 2 * BLOCK), F32)], axis=1)


def bias_line_grads(grad_lines):
    parts = grad_lines[:, :6].reshape(HEADS, 3, 2 * BLOCK)
    total = jnp.zeros((HEADS, SEQ + BLOCK), F32)
    for part in range(3):
        middle = REACH - part * BLOCK
        line = jnp.concatenate([parts[:, part, BLOCK:], parts[:, part, :BLOCK]], axis=1)
        total = total + jnp.pad(line, ((0, 0), (middle - BLOCK, SEQ - middle)))
    return total[:, BLOCK:]


FF_HALF = FF // 2
FF_BLOCK = 512
SLOTS = EXPERTS * CAP


def hidden_half(rows_ref, dout_ref, w_in_ref, w_out_ref, act_ref, dhid_ref, out_acc, drow_acc):
    def step(index, carry):
        cols = pl.ds(pl.multiple_of(index * FF_BLOCK, FF_BLOCK), FF_BLOCK)
        w_in = w_in_ref[:, cols]
        w_out = w_out_ref[cols, :]
        hidden = dot_nn(rows_ref[...], w_in)
        grad_act = dot_nt(dout_ref[...], w_out)
        square = hidden * hidden
        bend = jnp.tanh(hidden * (GELU_ROOT + (GELU_ROOT * GELU_CUBE) * square))
        half = 0.5 + 0.5 * bend
        act = (hidden * half).astype(BF16)
        slope = half + 0.5 * hidden * (1.0 - bend * bend) * (
            GELU_ROOT + (3.0 * GELU_ROOT * GELU_CUBE) * square
        )
        dhid = (grad_act * slope).astype(BF16)
        act_ref[:, cols] = act
        dhid_ref[:, cols] = dhid
        out_acc[...] += dot_nn(act, w_out)
        drow_acc[...] += dot_nt(dhid, w_in)
        return carry

    lax.fori_loop(0, FF_HALF // FF_BLOCK, step, 0)


def route_gates(logits, hits):
    shifted = jnp.exp(logits - jnp.max(logits, axis=0, keepdims=True))
    prob_all = shifted / jnp.sum(shifted, axis=0, keepdims=True)
    chosen_sum = jnp.sum(hits * prob_all, axis=0, keepdims=True)
    return prob_all, chosen_sum, hits * prob_all / chosen_sum


def pick_slots(key_row):
    slot = lax.broadcasted_iota(jnp.int32, (CAP, SEQ), 0).astype(F32)
    return key_row == slot


def first_half_kernel(
    act_one_ref, act_two_ref, cot_one_ref, cot_two_ref, key_ref, router_ref, mine_ref, w_in_ref, w_out_ref, *rest
):
    rows_ref, graw_ref, dout_ref, gcol_ref, act_ref, dhid_ref, out_acc, drow_acc = rest[-8:]

    def dispatch(index, act_part, cot_part):
        keys = key_ref[index * EXPERTS : (index + 1) * EXPERTS, :]
        logits = dot_nt(router_ref[...], act_part[...])[:EXPERTS, :]
        _, _, gate_rows = route_gates(logits, jnp.where(keys >= 0.0, 1.0, 0.0))
        mine = mine_ref[...] > 0.0
        picks = pick_slots(jnp.sum(jnp.where(mine, keys, 0.0), axis=0, keepdims=True))
        gate_row = jnp.sum(jnp.where(mine, gate_rows, 0.0), axis=0, keepdims=True)
        gates = jnp.sum(jnp.where(picks, gate_row, 0.0), axis=1, keepdims=True)
        chosen = jnp.where(picks, 1.0, 0.0).astype(BF16)
        rows_ref[...] = dot_nn(chosen, act_part[...]).astype(BF16)
        grads = dot_nn(chosen, cot_part[...])
        graw_ref[...] = grads.astype(BF16)
        dout_ref[...] = (gates * grads).astype(BF16)
        gcol_ref[...] = gates

    @pl.when(pl.program_id(0) == 0)
    def _():
        dispatch(0, act_one_ref, cot_one_ref)

    @pl.when(pl.program_id(0) == 1)
    def _():
        dispatch(1, act_two_ref, cot_two_ref)

    out_acc[...] = jnp.zeros_like(out_acc)
    drow_acc[...] = jnp.zeros_like(drow_acc)
    hidden_half(rows_ref, dout_ref, w_in_ref, w_out_ref, act_ref, dhid_ref, out_acc, drow_acc)


def second_half_kernel(
    rows_ref, graw_ref, dout_ref, gcol_ref, out_in, drow_in, key_ref, w_in_ref, w_out_ref, *rest
):
    act_ref, dhid_ref, out_ref, drow_ref, dgate_ref, out_acc, drow_acc = rest[-7:]
    out_acc[...] = out_in[...]
    drow_acc[...] = drow_in[...]
    hidden_half(rows_ref, dout_ref, w_in_ref, w_out_ref, act_ref, dhid_ref, out_acc, drow_acc)
    outs = out_acc[...]
    out_ref[...] = (gcol_ref[...] * outs).astype(BF16)
    drow_ref[...] = drow_acc[...].astype(BF16)
    dgates = jnp.sum(graw_ref[...].astype(F32) * outs, axis=1, keepdims=True)
    for index in range(2):

        @pl.when(pl.program_id(0) == index)
        def _():
            picks = pick_slots(key_ref[index : index + 1, :])
            dgate_ref[index : index + 1, :] = jnp.sum(jnp.where(picks, dgates, 0.0), axis=0, keepdims=True)


ANY_SPEC = pl.BlockSpec(memory_space=pl.ANY)


def place_kernel(order_ref, *refs):
    out_ref = refs[-1]
    for index, block in enumerate(refs[:-1]):
        out_ref[order_ref[index]] = block[...]


def place_blocks(order, blocks):
    shape = blocks[0].shape
    vmem = pl.BlockSpec(memory_space=pltpu.VMEM)
    return pl.pallas_call(
        place_kernel,
        in_specs=[pl.BlockSpec(memory_space=pltpu.SMEM)] + [vmem] * len(blocks),
        out_specs=vmem,
        out_shape=jax.ShapeDtypeStruct((len(blocks),) + shape, blocks[0].dtype),
        compiler_params=pltpu.CompilerParams(vmem_limit_bytes=32 * MIB),
        cost_estimate=cost(0, 4 * len(blocks) * shape[0] * shape[1]),
        name="place_blocks",
    )(order, *blocks)


ROW_BLOCK = 256


def picked_sum(key_ref, parts):
    slot = lax.broadcasted_iota(jnp.int32, (ROW_BLOCK, CAP), 1).astype(F32)
    total = None
    for index, part in enumerate(parts):
        picks = jnp.where(key_ref[:, index : index + 1] == slot, 1.0, 0.0).astype(BF16)
        rows = dot_nn(picks, part[...])
        total = rows if total is None else total + rows
    return total


def mix_kernel(key_ref, base_ref, one_ref, two_ref, three_ref, four_ref, out_ref):
    total = picked_sum(key_ref, (one_ref, two_ref, three_ref, four_ref))
    out_ref[...] = (base_ref[...] + total).astype(BF16)


def row_spec(width):
    return pl.BlockSpec((ROW_BLOCK, width), lambda step: (step, 0))


def mix_rows(keys, base, parts):
    return pl.pallas_call(
        mix_kernel,
        grid=(SEQ // ROW_BLOCK,),
        in_specs=[row_spec(EXPERTS), row_spec(D)] + [fixed_spec((CAP, D))] * EXPERTS,
        out_specs=row_spec(D),
        out_shape=jax.ShapeDtypeStruct((SEQ, D), BF16),
        compiler_params=pltpu.CompilerParams(vmem_limit_bytes=32 * MIB),
        cost_estimate=cost(2 * SEQ * SLOTS * D, 2 * SLOTS * D + 6 * SEQ * D),
        name="mix_rows",
    )(keys, base, *parts)


def norm_back(values, grad_norm, gain):
    inv_rms = lax.rsqrt(jnp.mean(values * values, axis=-1, keepdims=True) + NORM_EPSILON)
    unit_rows = values * inv_rms
    grad_gain = jnp.sum(grad_norm * unit_rows, axis=0, keepdims=True)
    grad_unit = grad_norm * gain
    middle = jnp.mean(grad_unit * unit_rows, axis=-1, keepdims=True)
    return inv_rms * (grad_unit - unit_rows * middle), grad_gain


def token_back_kernel(
    key_ref, extra_ref, residual_ref, cot_ref, attended_ref, gain_ref, weight_ref,
    one_ref, two_ref, three_ref, four_ref,
    grad_ref, dattended_ref, dweight_ref, dgain_ref, dweight_acc,
):
    step = pl.program_id(0)

    @pl.when(step == 0)
    def _():
        dweight_acc[...] = jnp.zeros_like(dweight_acc)
        dgain_ref[...] = jnp.zeros_like(dgain_ref)

    grad_act = extra_ref[...] + picked_sum(key_ref, (one_ref, two_ref, three_ref, four_ref))
    grad_norm, grad_gain = norm_back(residual_ref[...], grad_act, gain_ref[...])
    grad_rows = cot_ref[...].astype(F32) + grad_norm
    grad_ref[...] = grad_rows
    dgain_ref[...] += grad_gain
    branch = grad_rows.astype(BF16)
    dattended_ref[...] = dot_nt(branch, weight_ref[...]).astype(BF16)
    dweight_acc[...] += lax.dot_general(
        attended_ref[...], branch, (((0,), (0,)), ((), ())), preferred_element_type=F32
    )

    @pl.when(step == SEQ // ROW_BLOCK - 1)
    def _():
        dweight_ref[...] = dweight_acc[...].astype(BF16)


def token_back(keys, extra, residual, cotangent, attended, gain, packed, parts):
    return pl.pallas_call(
        token_back_kernel,
        grid=(SEQ // ROW_BLOCK,),
        in_specs=[row_spec(EXPERTS), row_spec(D), row_spec(D), row_spec(D), row_spec(D)]
        + [fixed_spec((1, D)), pl.BlockSpec((D, D), lambda step: (0, 3), pipeline_mode=pl.Buffered(1))]
        + [fixed_spec((CAP, D))] * EXPERTS,
        out_specs=[row_spec(D), row_spec(D), fixed_spec((D, D)), fixed_spec((1, D))],
        out_shape=[
            jax.ShapeDtypeStruct((SEQ, D), F32),
            jax.ShapeDtypeStruct((SEQ, D), BF16),
            jax.ShapeDtypeStruct((D, D), BF16),
            jax.ShapeDtypeStruct((1, D), F32),
        ],
        scratch_shapes=[pltpu.VMEM((D, D), F32)],
        compiler_params=pltpu.CompilerParams(vmem_limit_bytes=40 * MIB),
        cost_estimate=cost(2 * SEQ * (SLOTS + 2 * D) * D, 2 * SLOTS * D + 18 * SEQ * D),
        name="token_back",
    )(keys, extra, residual, cotangent, attended, gain, packed, *parts)


def qkv_back_kernel(
    act_ref, split_ref, weight_ref, token_ref, gain_ref, grad_ref,
    dweight_ref, dtoken_ref, dgain_ref, act_t, total,
):
    step = pl.program_id(0)

    @pl.when(step == 0)
    def _():
        act_t[...] = act_ref[...].T
        total[...] = jnp.zeros_like(total)

    split = split_ref[0]
    dweight_ref[...] = dot_nn(act_t[...], split).astype(BF16)
    total[...] += dot_nt(split, weight_ref[...])

    @pl.when(step == 2)
    def _():
        grad_norm, grad_gain = norm_back(token_ref[...].astype(F32), total[...], gain_ref[...])
        dtoken_ref[...] = (grad_ref[...] + grad_norm).astype(BF16)
        dgain_ref[...] = grad_gain


def qkv_back(act_one, grad_split, packed, tokens, gain, grad_residual):
    return pl.pallas_call(
        qkv_back_kernel,
        grid=(3,),
        in_specs=[
            fixed_spec((SEQ, D)),
            pl.BlockSpec((1, SEQ, D), lambda step: (step, 0, 0)),
            pl.BlockSpec((D, D), lambda step: (0, step)),
            fixed_spec((SEQ, D)),
            fixed_spec((1, D)),
            fixed_spec((SEQ, D)),
        ],
        out_specs=[pl.BlockSpec((D, D), lambda step: (0, step)), fixed_spec((SEQ, D)), fixed_spec((1, D))],
        out_shape=[
            jax.ShapeDtypeStruct((D, 3 * D), BF16),
            jax.ShapeDtypeStruct((SEQ, D), BF16),
            jax.ShapeDtypeStruct((1, D), F32),
        ],
        scratch_shapes=[pltpu.VMEM((D, SEQ), BF16), pltpu.VMEM((SEQ, D), F32)],
        compiler_params=pltpu.CompilerParams(vmem_limit_bytes=48 * MIB),
        cost_estimate=cost(12 * SEQ * D * D, 16 * SEQ * D + 12 * D * D),
        name="qkv_back",
    )(act_one, grad_split, packed, tokens, gain, grad_residual)


def slot_spec(pair, width):
    return pl.BlockSpec((CAP, width), lambda step: (2 * pair + step, 0))


def fixed_spec(shape, row=0):
    return pl.BlockSpec(shape, lambda step: (row, 0), pipeline_mode=pl.Buffered(1))


def expert_cost():
    return cost(16 * CAP * D * FF_HALF, 4 * D * FF_HALF + 20 * CAP * D)


def expert_first(pair, acts, cots, keys, router_rows, mine, w_in, w_out, earlier):
    widths = [(D, BF16), (D, BF16), (D, BF16), (1, F32), (FF_HALF, BF16), (FF_HALF, BF16), (D, F32), (D, F32)]
    inputs = [acts[0], acts[1], cots[0], cots[1], keys, router_rows, mine, w_in, w_out]
    return pl.pallas_call(
        first_half_kernel,
        grid=(2,),
        in_specs=[fixed_spec((SEQ, D))] * 4
        + [fixed_spec((2 * EXPERTS, SEQ)), fixed_spec((2 * EXPERTS, D)), fixed_spec((EXPERTS, 1))]
        + [fixed_spec((D, FF_HALF)), fixed_spec((FF_HALF, D))]
        + [ANY_SPEC] * len(earlier),
        out_specs=[slot_spec(pair, width) for width, _ in widths],
        out_shape=[jax.ShapeDtypeStruct((SLOTS, width), kind) for width, kind in widths],
        input_output_aliases={len(inputs) + i: i for i in range(len(earlier))},
        compiler_params=pltpu.CompilerParams(vmem_limit_bytes=56 * MIB),
        cost_estimate=expert_cost(),
        name="expert_first",
    )(*inputs, *earlier)


def expert_second(pair, first, keys, w_in, w_out, earlier):
    rows, graw, dout, gcol, _, _, outs, drows = first
    wide = jax.ShapeDtypeStruct((SLOTS, FF_HALF), BF16)
    narrow = jax.ShapeDtypeStruct((2 * CAP, D), BF16)
    inputs = [rows, graw, dout, gcol, outs, drows, keys, w_in, w_out]
    return pl.pallas_call(
        second_half_kernel,
        grid=(2,),
        in_specs=[slot_spec(pair, width) for width in (D, D, D, 1, D, D)]
        + [fixed_spec((2, SEQ)), fixed_spec((D, FF_HALF)), fixed_spec((FF_HALF, D), 1)]
        + [ANY_SPEC] * len(earlier),
        out_specs=[slot_spec(pair, FF_HALF)] * 2 + [slot_spec(0, D)] * 2 + [fixed_spec((8, SEQ))],
        out_shape=[wide, wide, narrow, narrow, jax.ShapeDtypeStruct((8, SEQ), F32)],
        input_output_aliases={len(inputs) + i: i for i in range(len(earlier))},
        scratch_shapes=[pltpu.VMEM((CAP, D), F32), pltpu.VMEM((CAP, D), F32)],
        compiler_params=pltpu.CompilerParams(vmem_limit_bytes=56 * MIB),
        cost_estimate=expert_cost(),
        name="expert_second",
    )(*inputs, *earlier)


def body(
    dp_size, tokens, segment_ids, routes, buckets, norm1_gain, w_qkv, w_attn_out, bias_table,
    norm2_gain, router, w_in, w_expert_out, cotangent,
):
    shard_rows = w_qkv.shape[0]
    table_rows = bias_table.shape[0]
    me = lax.axis_index("dp") % EXPERTS

    def swap(value, relation):
        if relation == 0:
            return value
        return lax.ppermute(value, "dp", [(i, i ^ relation) for i in range(dp_size)])

    across_x = (D // shard_rows) // DEEP
    shard_id = lax.axis_index("shard")
    my_z, my_x = shard_id // across_x, shard_id % across_x

    def step_z(value, step):
        pairs = [
            (z * across_x + x, (z + step) % DEEP * across_x + x) for z in range(DEEP) for x in range(across_x)
        ]
        return lax.ppermute(value, "shard", pairs)

    def step_x(value, step):
        pairs = [
            (z * across_x + x, z * across_x + (x + step) % across_x) for z in range(DEEP) for x in range(across_x)
        ]
        return lax.ppermute(value, "shard", pairs)

    def gather_rows(value):
        pieces = {}
        for back in range(DEEP):
            pieces[back, 0] = value if back == 0 else step_z(value, back)
            for side in range(1, across_x):
                pieces[back, side] = step_x(pieces[back, 0], side)
        order, blocks = [], []
        for (back, side), block in pieces.items():
            order.append((my_z - back) % DEEP * across_x + (my_x - side) % across_x)
            blocks.append(block)
        return place_blocks(jnp.stack(order).astype(jnp.int32), blocks)

    def sum_over_x(value):
        value = value.reshape(DEEP, across_x, -1, value.shape[-1])
        total = lax.dynamic_index_in_dim(value, my_x, 1, keepdims=False).astype(F32)
        for step in range(1, across_x):
            sent = lax.dynamic_index_in_dim(value, (my_x + step) % across_x, 1, keepdims=False)
            total = total + step_x(sent, step).astype(F32)
        return total.astype(BF16)

    def sum_over_z(value):
        total = lax.dynamic_index_in_dim(value, my_z, 0, keepdims=False).astype(F32)
        for step in range(1, DEEP):
            sent = lax.dynamic_index_in_dim(value, (my_z + step) % DEEP, 0, keepdims=False)
            total = total + step_z(sent, step).astype(F32)
        return total

    def after(values, earlier):
        return lax.optimization_barrier((values, earlier))[0]

    def spread(value):
        across = swap(value, 2)
        return [value, swap(value, 1), across, swap(across, 1)]

    table_col = jnp.pad(bias_table.reshape(-1), (0, shard_rows - table_rows * HEADS))
    small = jnp.concatenate(
        [norm1_gain[:, None], norm2_gain[:, None], router, table_col[:, None]], axis=1
    )
    packed = jnp.concatenate([w_qkv, w_attn_out, jnp.pad(small, ((0, 0), (0, 121)))], axis=1)
    core = lax.axis_index("dp") % 2
    core_rows = shard_rows // 2
    mine = lax.dynamic_slice_in_dim(packed, core * core_rows, core_rows, 0)
    mine = gather_rows(mine)
    other = swap(mine, 1)
    first_rows = jnp.where(core == 0, mine, other)[:, None]
    last_rows = jnp.where(core == 0, other, mine)[:, None]
    packed = jnp.concatenate([first_rows, last_rows], axis=1).reshape(D, mine.shape[2])
    qkv_weight = packed[:, : 3 * D]
    attn_weight = packed[:, 3 * D : 4 * D]
    gain_one = packed[:, 4 * D].astype(F32)
    gain_two = packed[:, 4 * D + 1].astype(F32)
    router_weight = packed[:, 4 * D + 2 : 4 * D + 6]
    bias_full = packed[:, 4 * D + 6].reshape(-1, shard_rows)[:, : table_rows * HEADS].reshape(BUCKETS, HEADS)

    my_in = lax.dynamic_index_in_dim(w_in, me, 0, keepdims=False)
    my_out = lax.dynamic_index_in_dim(w_expert_out, me, 0, keepdims=False)
    half_in = [lax.all_gather(my_in[:, :FF_HALF], "shard", axis=0, tiled=True)]
    full_out = lax.all_gather(my_out, "shard", axis=0, tiled=True)
    half_in.append(lax.all_gather(my_in[:, FF_HALF:], "shard", axis=0, tiled=True))

    cot_parts = spread(cotangent)

    expert_ids = jnp.arange(EXPERTS, dtype=jnp.int32)
    hits = (
        (routes[:, 0][None, :] == expert_ids[:, None]) | (routes[:, 1][None, :] == expert_ids[:, None])
    ).astype(F32)
    token_ids = jnp.arange(SEQ, dtype=jnp.int32)
    before = (token_ids[:, None] < token_ids[None, :]).astype(BF16)
    places = jnp.dot(hits.astype(BF16), before, preferred_element_type=F32)
    keys = jnp.where(hits > 0, places, -1.0)
    relation_ids = me ^ expert_ids

    def related(rows):
        return [lax.dynamic_index_in_dim(rows, relation_ids[x], 0, keepdims=False) for x in range(EXPERTS)]

    my_keys = related(keys)
    all_keys = spread(keys)
    their_keys = [lax.dynamic_index_in_dim(rows, me, 0, keepdims=False) for rows in all_keys]
    mine_col = (expert_ids == me).astype(F32)[:, None]
    key_cols = jnp.stack(my_keys, axis=1)

    bucket_hits = (jnp.arange(BUCKETS, dtype=jnp.int32)[:, None] == buckets[None, :]).astype(BF16)
    bias_vec = lax.dot_general(bias_full, bucket_hits, (((0,), (0,)), ((), ())), preferred_element_type=F32)
    lines = bias_lines(bias_vec)
    seg_col, seg_row = segment_ids[:, None], segment_ids[None, :]

    token_rows = tokens.astype(F32)
    unit_one, inv_one, normed_one = norm_forward(token_rows, gain_one)
    act_one = normed_one.astype(BF16)
    qkv_rows = jnp.dot(act_one, qkv_weight, preferred_element_type=F32).astype(BF16)
    attended, totals = attend_forward(qkv_rows, seg_col, seg_row, lines)
    residual = token_rows + jnp.dot(attended, attn_weight, preferred_element_type=F32)
    unit_two, inv_two, normed_two = norm_forward(residual, gain_two)
    act_two = normed_two.astype(BF16)
    act_parts = spread(act_two)

    logits = lax.dot_general(router_weight, act_two, (((0,), (1,)), ((), ())), preferred_element_type=F32)
    prob_all, chosen_sum, gates = route_gates(logits, hits)

    key_pairs = [jnp.stack(their_keys[:2]), jnp.stack(their_keys[2:])]
    all_pairs = [jnp.concatenate(all_keys[:2], axis=0), jnp.concatenate(all_keys[2:], axis=0)]
    router_rows = jnp.pad(router_weight.T, ((0, EXPERTS), (0, 0)))
    first = []
    for pair in range(2):
        here = slice(2 * pair, 2 * pair + 2)
        first = expert_first(
            pair, act_parts[here], cot_parts[here], all_pairs[pair], router_rows, mine_col, half_in[0], full_out, first
        )
    rows, _, dout, _, act_first, dhid_first, _, _ = first

    def weight_grad(left, right):
        return lax.dot_general(left, right, (((0,), (0,)), ((), ())), preferred_element_type=F32).astype(BF16)

    grad_in_first = weight_grad(rows, dhid_first)
    sum_in_first = lax.psum_scatter(grad_in_first, "shard", scatter_dimension=0, tiled=True)
    far = expert_second(1, first, after(key_pairs[1], grad_in_first), half_in[1], full_out, [])
    near = expert_second(0, first, key_pairs[0], half_in[1], full_out, far[:2])
    act_second, dhid_second = near[:2]
    dgate_parts = [swap(row, x) for x, row in enumerate([near[4][0], near[4][1], far[4][0], far[4][1]])]
    across_one = swap(far[3][:CAP], 2)
    across_two = swap(far[3][CAP:], 2)

    act_first, act_second = after((act_first, act_second), across_one)
    grad_out = jnp.concatenate([weight_grad(act_first, dout), weight_grad(act_second, dout)], axis=0)
    sum_out = lax.psum_scatter(grad_out, "shard", scatter_dimension=0, tiled=True)
    grad_in_second = weight_grad(rows, after(dhid_second, (grad_out, across_two, sum_in_first)))
    sum_in_second = lax.psum_scatter(grad_in_second, "shard", scatter_dimension=0, tiled=True)

    def send_back(near_rows, across_one, across_two):
        return [near_rows[:CAP], swap(near_rows[CAP:], 1), across_one, swap(across_two, 1)]

    drow_parts = send_back(near[3], across_one, across_two)
    out_far = swap(after(far[2], across_two), 2)

    def place(values):
        if dp_size > EXPERTS:
            every = [
                jnp.sum(lax.all_gather(v, "dp", axis=0).astype(F32).reshape((-1, EXPERTS) + v.shape), axis=0)
                for v in values
            ]
            return jnp.concatenate(every, axis=2)
        parts = [jnp.concatenate(list(pieces), axis=1).astype(F32) for pieces in zip(*[spread(v) for v in values])]
        out = jnp.zeros((EXPERTS,) + parts[0].shape, F32)
        for x in range(EXPERTS):
            out = lax.dynamic_update_index_in_dim(out, parts[x], relation_ids[x], 0)
        return out

    grad_gates = jnp.stack(related(jnp.stack(dgate_parts, axis=0)), axis=0)
    weighted = jnp.sum(grad_gates * gates, axis=0, keepdims=True)
    grad_prob = hits * (grad_gates - weighted) / chosen_sum
    grad_logits = (prob_all * (grad_prob - jnp.sum(prob_all * grad_prob, axis=0, keepdims=True))).astype(BF16)
    grad_router = lax.dot_general(act_two, grad_logits, (((0,), (1,)), ((), ())), preferred_element_type=F32)
    extra = lax.dot_general(grad_logits, router_weight, (((0,), (1,)), ((), ())), preferred_element_type=F32)
    grad_residual, grad_attended, grad_attn_weight, grad_gain_two = token_back(
        key_cols, extra, residual, cotangent, attended, gain_two[None], packed, drow_parts
    )
    grad_attended = after(grad_attended, grad_in_second)
    grad_split, grad_lines = attend_backward(
        qkv_rows, attended, grad_attended, totals, seg_col, seg_row, lines
    )
    grad_split, out_far, sum_out = lax.optimization_barrier((grad_split, out_far, sum_out))
    grad_qkv_weight, grad_tokens, grad_gain_one = qkv_back(
        act_one, grad_split, packed, tokens, gain_one[None], grad_residual
    )
    mixed_out = mix_rows(key_cols, residual, send_back(near[2], out_far[:CAP], out_far[CAP:]))
    grad_w_out = place([sum_out])
    grad_table = lax.dot_general(
        bucket_hits.astype(F32), bias_line_grads(grad_lines), (((1,), (1,)), ((), ())), precision=HIGHEST
    )
    shards = D // shard_rows
    table_sums = jnp.pad(
        grad_table.reshape(shards, table_rows * HEADS), ((0, 0), (0, shard_rows - table_rows * HEADS))
    ).reshape(D, 1)
    small = jnp.concatenate([grad_gain_one.T, grad_gain_two.T, grad_router, table_sums], axis=1)
    packed = jnp.concatenate(
        [grad_qkv_weight, grad_attn_weight, jnp.pad(small, ((0, 0), (0, 121))).astype(BF16)],
        axis=1,
    )
    packed = packed.reshape(shards, 2, core_rows, packed.shape[1])
    kept = lax.dynamic_index_in_dim(packed, core, 1, keepdims=False)
    sent = lax.dynamic_index_in_dim(packed, 1 - core, 1, keepdims=False)
    kept = (kept.astype(F32) + swap(sent, 1).astype(F32)).astype(BF16)
    kept, mixed_out, grad_tokens, grad_w_out = lax.optimization_barrier(
        (sum_over_x(kept), mixed_out, grad_tokens, grad_w_out)
    )
    kept, sum_in_second = lax.optimization_barrier((sum_over_z(kept), sum_in_second))
    grad_w_in = place([sum_in_first, sum_in_second])
    if dp_size > EXPERTS:
        total = lax.all_gather(kept, "dp", axis=0).reshape((-1, 2) + kept.shape)
        total = jnp.sum(lax.dynamic_index_in_dim(total, core, 1, keepdims=False), axis=0)
    else:
        kept = kept.astype(BF16)
        total = kept.astype(F32) + swap(kept, 2).astype(F32)
    other = swap(total, 1)
    packed = jnp.concatenate([jnp.where(core == 0, total, other), jnp.where(core == 0, other, total)], axis=0)
    return (
        mixed_out,
        grad_tokens,
        packed[:, 4 * D],
        packed[:, : 3 * D],
        packed[:, 3 * D : 4 * D],
        packed[:, 4 * D + 6][: table_rows * HEADS].reshape(table_rows, HEADS),
        packed[:, 4 * D + 1],
        packed[:, 4 * D + 2 : 4 * D + 6],
        grad_w_in,
        grad_w_out,
    )


def solution(mesh):
    return jax.shard_map(
        functools.partial(body, mesh.shape["dp"]),
        mesh=mesh,
        in_specs=(
            P(("dp", "shard"), None),
            P(("dp", "shard")),
            P(("dp", "shard"), None),
            P(),
            P("shard"),
            P("shard", None),
            P("shard", None),
            P("shard", None),
            P("shard"),
            P("shard", None),
            P(None, "shard", None),
            P(None, "shard", None),
            P(("dp", "shard"), None),
        ),
        out_specs=(
            P(("dp", "shard"), None),
            P(("dp", "shard"), None),
            P("shard"),
            P("shard", None),
            P("shard", None),
            P("shard", None),
            P("shard"),
            P("shard", None),
            P(None, "shard", None),
            P(None, "shard", None),
        ),
        check_vma=False,
    )
```

```python
import functools

import jax
import jax.numpy as jnp
from jax import lax
from jax.experimental import pallas as pl
from jax.experimental.pallas import tpu as pltpu
from jax.sharding import PartitionSpec as P

D = 768
HEADS = 12
HEAD_DIM = 64
FF = 3072
EXPERTS = 4
BUCKETS = 32
SEQ = 1024
CAP = 640
DEEP = 4
BLOCK = 256
REACH = 768
NORM_EPSILON = 1e-06
HIGHEST = lax.Precision.HIGHEST
NEG = -1e30
COST_CUT = 256
F32 = jnp.float32
BF16 = jnp.bfloat16
MIB = 1024 * 1024
GELU_ROOT = 0.7978845608028654
GELU_CUBE = 0.044715


def norm_forward(values, gain_vec):
    inv_rms = lax.rsqrt(jnp.mean(values * values, axis=-1, keepdims=True) + NORM_EPSILON)
    unit_rows = values * inv_rms
    return unit_rows, inv_rms, unit_rows * gain_vec


def cost(flops, moved):
    return pl.CostEstimate(flops=flops // COST_CUT, bytes_accessed=moved // COST_CUT, transcendentals=0)


def key_span(block):
    low = max(0, (block + 1) * BLOCK - REACH)
    return low, (block + 1) * BLOCK - low


def fill_mask(seg_col_ref, seg_row_ref, mask_ref):
    for block in range(SEQ // BLOCK):
        low, width = key_span(block)
        same = (
            seg_col_ref[low : low + width, :]
            == seg_row_ref[:, block * BLOCK : (block + 1) * BLOCK]
        )
        mask_ref[block, REACH - width :, :] = jnp.where(same, 0.0, NEG)


def fill_bias(line_ref, bias_ref):
    for head in range(2):
        for part in range(3):
            rows = line_ref[0, 3 * head + part : 3 * head + part + 1, :]
            count = 1
            while count < BLOCK:
                rows = jnp.concatenate([rows, pltpu.roll(rows, count, 1)], axis=0)
                count *= 2
            bias_ref[head, part * BLOCK : (part + 1) * BLOCK, :] = rows[:, :BLOCK]


def diagonal_sums(square):
    rows = jnp.concatenate([square, jnp.zeros_like(square)], axis=1)
    count = BLOCK
    while count > 1:
        count //= 2
        rows = rows[:count] + pltpu.roll(rows[count:], 2 * BLOCK - count, 1)
    return rows


def head_lanes(head, rows):
    lane = lax.broadcasted_iota(jnp.int32, rows.shape, 1)
    return jnp.where(lane // HEAD_DIM == head, rows, jnp.zeros_like(rows))


def dot_nt(left, right):
    return lax.dot_general(left, right, (((1,), (1,)), ((), ())), preferred_element_type=F32)


def dot_nn(left, right):
    return jnp.dot(left, right, preferred_element_type=F32)


def attention_kernel(
    q_ref, k_ref, v_ref, seg_col_ref, seg_row_ref, line_ref, out_ref, total_ref, mask_ref, bias_ref
):
    @pl.when(pl.program_id(0) == 0)
    def _():
        fill_mask(seg_col_ref, seg_row_ref, mask_ref)

    fill_bias(line_ref, bias_ref)
    values_t = v_ref[...].T
    for block in range(SEQ // BLOCK):
        low, width = key_span(block)
        here = slice(block * BLOCK, (block + 1) * BLOCK)
        queries = q_ref[here, :] * jnp.asarray(HEAD_DIM**-0.5, BF16)
        parts = []
        for head in range(2):
            scores = dot_nt(k_ref[low : low + width, :], head_lanes(head, queries))
            scores = scores + bias_ref[head, REACH - width :, :] + mask_ref[block, REACH - width :, :]
            top = jnp.max(scores, axis=0, keepdims=True)
            weights = jnp.exp(scores - top)
            denom = jnp.sum(weights, axis=0, keepdims=True)
            mixed = dot_nn(values_t[:, low : low + width], weights.astype(BF16))
            parts.append(mixed[head * HEAD_DIM : (head + 1) * HEAD_DIM, :] / denom)
            total_ref[0, head : head + 1, here] = top + jnp.log(denom)
        out_ref[here, :] = jnp.concatenate(parts, axis=0).T.astype(BF16)


def attention_back_kernel(
    q_ref, k_ref, v_ref, out_ref, grad_ref, total_ref, seg_col_ref, seg_row_ref, line_ref,
    dqkv_ref, dline_ref, mask_ref, bias_ref, dbias_ref, dk_ref, dv_ref,
):
    @pl.when(pl.program_id(0) == 0)
    def _():
        fill_mask(seg_col_ref, seg_row_ref, mask_ref)

    fill_bias(line_ref, bias_ref)
    keys_t = k_ref[...].T
    dk_ref[...] = jnp.zeros_like(dk_ref)
    dv_ref[...] = jnp.zeros_like(dv_ref)
    dbias_ref[...] = jnp.zeros_like(dbias_ref)
    scale = HEAD_DIM**-0.5
    for block in range(SEQ // BLOCK):
        low, width = key_span(block)
        here = slice(block * BLOCK, (block + 1) * BLOCK)
        span = slice(low, low + width)
        queries = q_ref[here, :] * jnp.asarray(scale, BF16)
        grads = grad_ref[here, :]
        inner = (grads.astype(F32) * out_ref[here, :].astype(F32)).T
        parts = []
        for head in range(2):
            rows = slice(head * HEAD_DIM, (head + 1) * HEAD_DIM)
            query_head = head_lanes(head, queries)
            grad_head = head_lanes(head, grads)
            scores = dot_nt(k_ref[span, :], query_head)
            scores = scores + bias_ref[head, REACH - width :, :] + mask_ref[block, REACH - width :, :]
            probs = jnp.exp(scores - total_ref[0, head : head + 1, here])
            grad_probs = dot_nt(v_ref[span, :], grad_head)
            delta = jnp.sum(inner[rows, :], axis=0, keepdims=True)
            grad_scores = probs * (grad_probs - delta)
            dbias_ref[head, REACH - width :, :] += grad_scores
            low_scores = grad_scores.astype(BF16)
            dv_ref[span, :] += dot_nn(probs.astype(BF16), grad_head)
            dk_ref[span, :] += dot_nn(low_scores, query_head)
            parts.append(dot_nn(keys_t[:, span], low_scores)[rows, :])
        dqkv_ref[0, here, :] = (jnp.concatenate(parts, axis=0).T * scale).astype(BF16)
    dqkv_ref[1, :, :] = dk_ref[...].astype(BF16)
    dqkv_ref[2, :, :] = dv_ref[...].astype(BF16)
    for head in range(2):
        for part in range(3):
            sums = diagonal_sums(dbias_ref[head, part * BLOCK : (part + 1) * BLOCK, :])
            dline_ref[0, 3 * head + part : 3 * head + part + 1, :] = sums
    dline_ref[0, 6:8, :] = jnp.zeros((2, 2 * BLOCK), F32)


def pair_spec(offset):
    return pl.BlockSpec((SEQ, 2 * HEAD_DIM), lambda pair: (0, pair + offset))


PAIRS = HEADS // 2
SEG_SPECS = [
    pl.BlockSpec((SEQ, 1), lambda pair: (0, 0)),
    pl.BlockSpec((1, SEQ), lambda pair: (0, 0)),
    pl.BlockSpec((1, 8, 2 * BLOCK), lambda pair: (pair, 0, 0)),
]
TOTAL_SPEC = pl.BlockSpec((1, 8, SEQ), lambda pair: (pair, 0, 0))
PAIR_SCRATCH = [
    pltpu.VMEM((SEQ // BLOCK, REACH, BLOCK), F32),
    pltpu.VMEM((2, REACH, BLOCK), F32),
]


def attend_forward(qkv_rows, seg_col, seg_row, lines):
    return pl.pallas_call(
        attention_kernel,
        grid=(PAIRS,),
        in_specs=[pair_spec(0), pair_spec(PAIRS), pair_spec(2 * PAIRS)] + SEG_SPECS,
        out_specs=[pair_spec(0), TOTAL_SPEC],
        out_shape=[
            jax.ShapeDtypeStruct((SEQ, D), BF16),
            jax.ShapeDtypeStruct((PAIRS, 8, SEQ), F32),
        ],
        scratch_shapes=PAIR_SCRATCH,
        compiler_params=pltpu.CompilerParams(vmem_limit_bytes=48 * MIB),
        cost_estimate=cost(4 * SEQ * SEQ * D, 8 * SEQ * D),
        name="attend_forward",
    )(qkv_rows, qkv_rows, qkv_rows, seg_col, seg_row, lines)


def attend_backward(qkv_rows, attended, grad_attended, totals, seg_col, seg_row, lines):
    return pl.pallas_call(
        attention_back_kernel,
        grid=(PAIRS,),
        in_specs=[
            pair_spec(0), pair_spec(PAIRS), pair_spec(2 * PAIRS), pair_spec(0), pair_spec(0), TOTAL_SPEC,
        ] + SEG_SPECS,
        out_specs=[
            pl.BlockSpec((3, SEQ, 2 * HEAD_DIM), lambda pair: (0, 0, pair)),
            pl.BlockSpec((1, 8, 2 * BLOCK), lambda pair: (pair, 0, 0)),
        ],
        out_shape=[
            jax.ShapeDtypeStruct((3, SEQ, D), BF16),
            jax.ShapeDtypeStruct((PAIRS, 8, 2 * BLOCK), F32),
        ],
        scratch_shapes=PAIR_SCRATCH + [
            pltpu.VMEM((2, REACH, BLOCK), F32),
            pltpu.VMEM((SEQ, 2 * HEAD_DIM), F32),
            pltpu.VMEM((SEQ, 2 * HEAD_DIM), F32),
        ],
        compiler_params=pltpu.CompilerParams(vmem_limit_bytes=48 * MIB),
        cost_estimate=cost(10 * SEQ * SEQ * D, 16 * SEQ * D),
        name="attend_backward",
    )(qkv_rows, qkv_rows, qkv_rows, attended, grad_attended, totals, seg_col, seg_row, lines)


def bias_lines(bias_vec):
    reach = jnp.concatenate([jnp.full((HEADS, BLOCK), NEG, F32), bias_vec], axis=1)
    parts = []
    for part in range(3):
        middle = REACH - part * BLOCK
        parts.append(
            jnp.concatenate([reach[:, middle : middle + BLOCK], reach[:, middle - BLOCK : middle]], axis=1)
        )
    lines = jnp.stack(parts, axis=1).reshape(PAIRS, 6, 2 * BLOCK)
    return jnp.concatenate([lines, jnp.zeros((PAIRS, 2, 2 * BLOCK), F32)], axis=1)


def bias_line_grads(grad_lines):
    parts = grad_lines[:, :6].reshape(HEADS, 3, 2 * BLOCK)
    total = jnp.zeros((HEADS, SEQ + BLOCK), F32)
    for part in range(3):
        middle = REACH - part * BLOCK
        line = jnp.concatenate([parts[:, part, BLOCK:], parts[:, part, :BLOCK]], axis=1)
        total = total + jnp.pad(line, ((0, 0), (middle - BLOCK, SEQ - middle)))
    return total[:, BLOCK:]


FF_HALF = FF // 2
FF_BLOCK = 1536
SLOTS = EXPERTS * CAP


def hidden_half(rows_ref, dout_ref, w_in_ref, w_out_ref, act_ref, dhid_ref, out_acc, drow_acc):
    def step(index, carry):
        cols = pl.ds(pl.multiple_of(index * FF_BLOCK, FF_BLOCK), FF_BLOCK)
        w_in = w_in_ref[:, cols]
        w_out = w_out_ref[cols, :]
        hidden = dot_nn(rows_ref[...], w_in)
        grad_act = dot_nt(dout_ref[...], w_out)
        square = hidden * hidden
        bend = jnp.tanh(hidden * (GELU_ROOT + (GELU_ROOT * GELU_CUBE) * square))
        half = 0.5 + 0.5 * bend
        act = (hidden * half).astype(BF16)
        slope = half + 0.5 * hidden * (1.0 - bend * bend) * (
            GELU_ROOT + (3.0 * GELU_ROOT * GELU_CUBE) * square
        )
        dhid = (grad_act * slope).astype(BF16)
        act_ref[:, cols] = act
        dhid_ref[:, cols] = dhid
        out_acc[...] += dot_nn(act, w_out)
        drow_acc[...] += dot_nt(dhid, w_in)
        return carry

    lax.fori_loop(0, FF_HALF // FF_BLOCK, step, 0)


def route_gates(logits, hits):
    shifted = jnp.exp(logits - jnp.max(logits, axis=0, keepdims=True))
    prob_all = shifted / jnp.sum(shifted, axis=0, keepdims=True)
    chosen_sum = jnp.sum(hits * prob_all, axis=0, keepdims=True)
    return prob_all, chosen_sum, hits * prob_all / chosen_sum


def pick_slots(key_row):
    slot = lax.broadcasted_iota(jnp.int32, (CAP, SEQ), 0).astype(F32)
    return key_row == slot


def first_half_kernel(
    act_one_ref, act_two_ref, cot_one_ref, cot_two_ref, key_ref, router_ref, mine_ref, w_in_ref, w_out_ref, *rest
):
    rows_ref, graw_ref, dout_ref, gcol_ref, act_ref, dhid_ref, out_acc, drow_acc = rest[-8:]

    def dispatch(index, act_part, cot_part):
        keys = key_ref[index * EXPERTS : (index + 1) * EXPERTS, :]
        logits = dot_nt(router_ref[...], act_part[...])[:EXPERTS, :]
        _, _, gate_rows = route_gates(logits, jnp.where(keys >= 0.0, 1.0, 0.0))
        mine = mine_ref[...] > 0.0
        picks = pick_slots(jnp.sum(jnp.where(mine, keys, 0.0), axis=0, keepdims=True))
        gate_row = jnp.sum(jnp.where(mine, gate_rows, 0.0), axis=0, keepdims=True)
        gates = jnp.sum(jnp.where(picks, gate_row, 0.0), axis=1, keepdims=True)
        chosen = jnp.where(picks, 1.0, 0.0).astype(BF16)
        rows_ref[...] = dot_nn(chosen, act_part[...]).astype(BF16)
        grads = dot_nn(chosen, cot_part[...])
        graw_ref[...] = grads.astype(BF16)
        dout_ref[...] = (gates * grads).astype(BF16)
        gcol_ref[...] = gates

    @pl.when(pl.program_id(0) == 0)
    def _():
        dispatch(0, act_one_ref, cot_one_ref)

    @pl.when(pl.program_id(0) == 1)
    def _():
        dispatch(1, act_two_ref, cot_two_ref)

    out_acc[...] = jnp.zeros_like(out_acc)
    drow_acc[...] = jnp.zeros_like(drow_acc)
    hidden_half(rows_ref, dout_ref, w_in_ref, w_out_ref, act_ref, dhid_ref, out_acc, drow_acc)


def second_half_kernel(
    rows_ref, graw_ref, dout_ref, gcol_ref, out_in, drow_in, key_ref, mine_ref, w_in_ref, w_out_ref, *rest
):
    act_ref, dhid_ref, out_ref, drow_ref, dgate_ref, out_acc, drow_acc = rest[-7:]
    out_acc[...] = out_in[...]
    drow_acc[...] = drow_in[...]
    hidden_half(rows_ref, dout_ref, w_in_ref, w_out_ref, act_ref, dhid_ref, out_acc, drow_acc)
    outs = out_acc[...]
    out_ref[...] = (gcol_ref[...] * outs).astype(BF16)
    drow_ref[...] = drow_acc[...].astype(BF16)
    dgates = jnp.sum(graw_ref[...].astype(F32) * outs, axis=1, keepdims=True)
    for index in range(2):

        @pl.when(pl.program_id(0) == index)
        def _():
            keys = key_ref[index * EXPERTS : (index + 1) * EXPERTS, :]
            picks = pick_slots(jnp.sum(jnp.where(mine_ref[...] > 0.0, keys, 0.0), axis=0, keepdims=True))
            dgate_ref[index : index + 1, :] = jnp.sum(jnp.where(picks, dgates, 0.0), axis=0, keepdims=True)


ANY_SPEC = pl.BlockSpec(memory_space=pl.ANY)


def place_kernel(order_ref, *refs):
    out_ref = refs[-1]
    for index, block in enumerate(refs[:-1]):
        out_ref[order_ref[index]] = block[...]


def place_blocks(order, blocks):
    shape = blocks[0].shape
    vmem = pl.BlockSpec(memory_space=pltpu.VMEM)
    return pl.pallas_call(
        place_kernel,
        in_specs=[pl.BlockSpec(memory_space=pltpu.SMEM)] + [vmem] * len(blocks),
        out_specs=vmem,
        out_shape=jax.ShapeDtypeStruct((len(blocks),) + shape, blocks[0].dtype),
        compiler_params=pltpu.CompilerParams(vmem_limit_bytes=32 * MIB),
        cost_estimate=cost(0, 4 * len(blocks) * shape[0] * shape[1]),
        name="place_blocks",
    )(order, *blocks)


ROW_BLOCK = 256


def picked_sum(key_ref, parts):
    slot = lax.broadcasted_iota(jnp.int32, (ROW_BLOCK, CAP), 1).astype(F32)
    total = None
    for index, part in enumerate(parts):
        picks = jnp.where(key_ref[:, index : index + 1] == slot, 1.0, 0.0).astype(BF16)
        rows = dot_nn(picks, part[...])
        total = rows if total is None else total + rows
    return total


def mix_kernel(key_ref, base_ref, one_ref, two_ref, three_ref, four_ref, out_ref):
    total = picked_sum(key_ref, (one_ref, two_ref, three_ref, four_ref))
    out_ref[...] = (base_ref[...] + total).astype(BF16)


def row_spec(width):
    return pl.BlockSpec((ROW_BLOCK, width), lambda step: (step, 0))


def mix_rows(keys, base, parts):
    return pl.pallas_call(
        mix_kernel,
        grid=(SEQ // ROW_BLOCK,),
        in_specs=[row_spec(EXPERTS), row_spec(D)] + [fixed_spec((CAP, D))] * EXPERTS,
        out_specs=row_spec(D),
        out_shape=jax.ShapeDtypeStruct((SEQ, D), BF16),
        compiler_params=pltpu.CompilerParams(vmem_limit_bytes=32 * MIB),
        cost_estimate=cost(2 * SEQ * SLOTS * D, 2 * SLOTS * D + 6 * SEQ * D),
        name="mix_rows",
    )(keys, base, *parts)


def norm_back(values, grad_norm, gain):
    inv_rms = lax.rsqrt(jnp.mean(values * values, axis=-1, keepdims=True) + NORM_EPSILON)
    unit_rows = values * inv_rms
    grad_gain = jnp.sum(grad_norm * unit_rows, axis=0, keepdims=True)
    grad_unit = grad_norm * gain
    middle = jnp.mean(grad_unit * unit_rows, axis=-1, keepdims=True)
    return inv_rms * (grad_unit - unit_rows * middle), grad_gain


def token_back_kernel(
    key_ref, extra_ref, residual_ref, cot_ref, attended_ref, gain_ref, weight_ref,
    one_ref, two_ref, three_ref, four_ref,
    grad_ref, dattended_ref, dweight_ref, dgain_ref, dweight_acc,
):
    step = pl.program_id(0)

    @pl.when(step == 0)
    def _():
        dweight_acc[...] = jnp.zeros_like(dweight_acc)
        dgain_ref[...] = jnp.zeros_like(dgain_ref)

    grad_act = extra_ref[...] + picked_sum(key_ref, (one_ref, two_ref, three_ref, four_ref))
    grad_norm, grad_gain = norm_back(residual_ref[...], grad_act, gain_ref[...])
    grad_rows = cot_ref[...].astype(F32) + grad_norm
    grad_ref[...] = grad_rows
    dgain_ref[...] += grad_gain
    branch = grad_rows.astype(BF16)
    dattended_ref[...] = dot_nt(branch, weight_ref[...]).astype(BF16)
    dweight_acc[...] += lax.dot_general(
        attended_ref[...], branch, (((0,), (0,)), ((), ())), preferred_element_type=F32
    )

    @pl.when(step == SEQ // ROW_BLOCK - 1)
    def _():
        dweight_ref[...] = dweight_acc[...].astype(BF16)


def token_back(keys, extra, residual, cotangent, attended, gain, packed, parts):
    return pl.pallas_call(
        token_back_kernel,
        grid=(SEQ // ROW_BLOCK,),
        in_specs=[row_spec(EXPERTS), row_spec(D), row_spec(D), row_spec(D), row_spec(D)]
        + [fixed_spec((1, D)), pl.BlockSpec((D, D), lambda step: (0, 3), pipeline_mode=pl.Buffered(1))]
        + [fixed_spec((CAP, D))] * EXPERTS,
        out_specs=[row_spec(D), row_spec(D), fixed_spec((D, D)), fixed_spec((1, D))],
        out_shape=[
            jax.ShapeDtypeStruct((SEQ, D), F32),
            jax.ShapeDtypeStruct((SEQ, D), BF16),
            jax.ShapeDtypeStruct((D, D), BF16),
            jax.ShapeDtypeStruct((1, D), F32),
        ],
        scratch_shapes=[pltpu.VMEM((D, D), F32)],
        compiler_params=pltpu.CompilerParams(vmem_limit_bytes=40 * MIB),
        cost_estimate=cost(2 * SEQ * (SLOTS + 2 * D) * D, 2 * SLOTS * D + 18 * SEQ * D),
        name="token_back",
    )(keys, extra, residual, cotangent, attended, gain, packed, *parts)


def qkv_back_kernel(
    act_ref, split_ref, weight_ref, token_ref, gain_ref, grad_ref,
    dweight_ref, dtoken_ref, dgain_ref, act_t, total,
):
    step = pl.program_id(0)

    @pl.when(step == 0)
    def _():
        act_t[...] = act_ref[...].T
        total[...] = jnp.zeros_like(total)

    split = split_ref[0]
    dweight_ref[...] = dot_nn(act_t[...], split).astype(BF16)
    total[...] += dot_nt(split, weight_ref[...])

    @pl.when(step == 2)
    def _():
        grad_norm, grad_gain = norm_back(token_ref[...].astype(F32), total[...], gain_ref[...])
        dtoken_ref[...] = (grad_ref[...] + grad_norm).astype(BF16)
        dgain_ref[...] = grad_gain


def qkv_back(act_one, grad_split, packed, tokens, gain, grad_residual):
    return pl.pallas_call(
        qkv_back_kernel,
        grid=(3,),
        in_specs=[
            fixed_spec((SEQ, D)),
            pl.BlockSpec((1, SEQ, D), lambda step: (step, 0, 0)),
            pl.BlockSpec((D, D), lambda step: (0, step)),
            fixed_spec((SEQ, D)),
            fixed_spec((1, D)),
            fixed_spec((SEQ, D)),
        ],
        out_specs=[pl.BlockSpec((D, D), lambda step: (0, step)), fixed_spec((SEQ, D)), fixed_spec((1, D))],
        out_shape=[
            jax.ShapeDtypeStruct((D, 3 * D), BF16),
            jax.ShapeDtypeStruct((SEQ, D), BF16),
            jax.ShapeDtypeStruct((1, D), F32),
        ],
        scratch_shapes=[pltpu.VMEM((D, SEQ), BF16), pltpu.VMEM((SEQ, D), F32)],
        compiler_params=pltpu.CompilerParams(vmem_limit_bytes=48 * MIB),
        cost_estimate=cost(12 * SEQ * D * D, 16 * SEQ * D + 12 * D * D),
        name="qkv_back",
    )(act_one, grad_split, packed, tokens, gain, grad_residual)


def slot_spec(pair, width):
    return pl.BlockSpec((CAP, width), lambda step: (2 * pair + step, 0))


def fixed_spec(shape, row=0):
    return pl.BlockSpec(shape, lambda step: (row, 0), pipeline_mode=pl.Buffered(1))


def expert_cost():
    return cost(16 * CAP * D * FF_HALF, 4 * D * FF_HALF + 20 * CAP * D)


def expert_first(pair, acts, cots, keys, router_rows, mine, w_in, w_out, earlier):
    widths = [(D, BF16), (D, BF16), (D, BF16), (1, F32), (FF_HALF, BF16), (FF_HALF, BF16), (D, F32), (D, F32)]
    inputs = [acts[0], acts[1], cots[0], cots[1], keys, router_rows, mine, w_in, w_out]
    return pl.pallas_call(
        first_half_kernel,
        grid=(2,),
        in_specs=[fixed_spec((SEQ, D))] * 4
        + [fixed_spec((2 * EXPERTS, SEQ)), fixed_spec((2 * EXPERTS, D)), fixed_spec((EXPERTS, 1))]
        + [fixed_spec((D, FF_HALF)), fixed_spec((FF_HALF, D))]
        + [ANY_SPEC] * len(earlier),
        out_specs=[slot_spec(pair, width) for width, _ in widths],
        out_shape=[jax.ShapeDtypeStruct((SLOTS, width), kind) for width, kind in widths],
        input_output_aliases={len(inputs) + i: i for i in range(len(earlier))},
        compiler_params=pltpu.CompilerParams(vmem_limit_bytes=56 * MIB),
        cost_estimate=expert_cost(),
        name="expert_first",
    )(*inputs, *earlier)


def expert_second(pair, first, keys, mine, w_in, w_out, earlier):
    rows, graw, dout, gcol, _, _, outs, drows = first
    wide = jax.ShapeDtypeStruct((SLOTS, FF_HALF), BF16)
    narrow = jax.ShapeDtypeStruct((2 * CAP, D), BF16)
    inputs = [rows, graw, dout, gcol, outs, drows, keys, mine, w_in, w_out]
    return pl.pallas_call(
        second_half_kernel,
        grid=(2,),
        in_specs=[slot_spec(pair, width) for width in (D, D, D, 1, D, D)]
        + [fixed_spec((2 * EXPERTS, SEQ)), fixed_spec((EXPERTS, 1))]
        + [fixed_spec((D, FF_HALF)), fixed_spec((FF_HALF, D), 1)]
        + [ANY_SPEC] * len(earlier),
        out_specs=[slot_spec(pair, FF_HALF)] * 2 + [slot_spec(0, D)] * 2 + [fixed_spec((8, SEQ))],
        out_shape=[wide, wide, narrow, narrow, jax.ShapeDtypeStruct((8, SEQ), F32)],
        input_output_aliases={len(inputs) + i: i for i in range(len(earlier))},
        scratch_shapes=[pltpu.VMEM((CAP, D), F32), pltpu.VMEM((CAP, D), F32)],
        compiler_params=pltpu.CompilerParams(vmem_limit_bytes=56 * MIB),
        cost_estimate=expert_cost(),
        name="expert_second",
    )(*inputs, *earlier)


def body(
    dp_size, tokens, segment_ids, routes, buckets, norm1_gain, w_qkv, w_attn_out, bias_table,
    norm2_gain, router, w_in, w_expert_out, cotangent,
):
    shard_rows = w_qkv.shape[0]
    table_rows = bias_table.shape[0]
    me = lax.axis_index("dp") % EXPERTS

    def swap(value, relation):
        if relation == 0:
            return value
        return lax.ppermute(value, "dp", [(i, i ^ relation) for i in range(dp_size)])

    across_x = (D // shard_rows) // DEEP
    shard_id = lax.axis_index("shard")
    my_z, my_x = shard_id // across_x, shard_id % across_x

    def step_z(value, step):
        pairs = [
            (z * across_x + x, (z + step) % DEEP * across_x + x) for z in range(DEEP) for x in range(across_x)
        ]
        return lax.ppermute(value, "shard", pairs)

    def step_x(value, step):
        pairs = [
            (z * across_x + x, z * across_x + (x + step) % across_x) for z in range(DEEP) for x in range(across_x)
        ]
        return lax.ppermute(value, "shard", pairs)

    def gather_rows(value):
        pieces = {}
        for back in range(DEEP):
            pieces[back, 0] = value if back == 0 else step_z(value, back)
            for side in range(1, across_x):
                pieces[back, side] = step_x(pieces[back, 0], side)
        order, blocks = [], []
        for (back, side), block in pieces.items():
            order.append((my_z - back) % DEEP * across_x + (my_x - side) % across_x)
            blocks.append(block)
        return place_blocks(jnp.stack(order).astype(jnp.int32), blocks)

    def parts_over_x(value):
        value = value.reshape(DEEP, across_x, -1, value.shape[-1])
        parts = [lax.dynamic_index_in_dim(value, my_x, 1, keepdims=False)]
        for step in range(1, across_x):
            sent = lax.dynamic_index_in_dim(value, (my_x + step) % across_x, 1, keepdims=False)
            parts.append(step_x(sent, step))
        return parts

    def parts_over_z(value):
        parts = [lax.dynamic_index_in_dim(value, my_z, 0, keepdims=False)]
        for step in range(1, DEEP):
            sent = lax.dynamic_index_in_dim(value, (my_z + step) % DEEP, 0, keepdims=False)
            parts.append(step_z(sent, step))
        return parts

    def add_parts(parts):
        total = parts[0].astype(F32)
        for part in parts[1:]:
            total = total + part.astype(F32)
        return total

    def sum_over_x(value):
        return add_parts(parts_over_x(value)).astype(BF16)

    def sum_over_z(value):
        return add_parts(parts_over_z(value))

    def after(values, earlier):
        return lax.optimization_barrier((values, earlier))[0]

    def spread(value):
        across = swap(value, 2)
        return [value, swap(value, 1), across, swap(across, 1)]

    table_col = jnp.pad(bias_table.reshape(-1), (0, shard_rows - table_rows * HEADS))
    small = jnp.concatenate(
        [norm1_gain[:, None], norm2_gain[:, None], router, table_col[:, None]], axis=1
    )
    packed = jnp.concatenate([w_qkv, w_attn_out, jnp.pad(small, ((0, 0), (0, 121)))], axis=1)
    core = lax.axis_index("dp") % 2
    core_rows = shard_rows // 2
    mine = lax.dynamic_slice_in_dim(packed, core * core_rows, core_rows, 0)
    mine = gather_rows(mine)
    other = swap(mine, 1)
    first_rows = jnp.where(core == 0, mine, other)[:, None]
    last_rows = jnp.where(core == 0, other, mine)[:, None]
    packed = jnp.concatenate([first_rows, last_rows], axis=1).reshape(D, mine.shape[2])
    qkv_weight = packed[:, : 3 * D]
    attn_weight = packed[:, 3 * D : 4 * D]
    gain_one = packed[:, 4 * D].astype(F32)
    gain_two = packed[:, 4 * D + 1].astype(F32)
    router_weight = packed[:, 4 * D + 2 : 4 * D + 6]
    bias_full = packed[:, 4 * D + 6].reshape(-1, shard_rows)[:, : table_rows * HEADS].reshape(BUCKETS, HEADS)

    my_in = lax.dynamic_index_in_dim(w_in, me, 0, keepdims=False)
    my_out = lax.dynamic_index_in_dim(w_expert_out, me, 0, keepdims=False)
    half_in = [lax.all_gather(my_in[:, :FF_HALF], "shard", axis=0, tiled=True)]
    full_out = lax.all_gather(my_out, "shard", axis=0, tiled=True)
    half_in.append(lax.all_gather(my_in[:, FF_HALF:], "shard", axis=0, tiled=True))

    cot_parts = spread(cotangent)

    expert_ids = jnp.arange(EXPERTS, dtype=jnp.int32)
    hits = (
        (routes[:, 0][None, :] == expert_ids[:, None]) | (routes[:, 1][None, :] == expert_ids[:, None])
    ).astype(F32)
    token_ids = jnp.arange(SEQ, dtype=jnp.int32)
    before = (token_ids[:, None] < token_ids[None, :]).astype(BF16)
    places = jnp.dot(hits.astype(BF16), before, preferred_element_type=F32)
    keys = jnp.where(hits > 0, places, -1.0)
    relation_ids = me ^ expert_ids

    def related(rows):
        chosen = (relation_ids[:, None] == expert_ids[None, :]).astype(F32)
        return jnp.sum(chosen[:, :, None] * rows[None], axis=1)

    all_keys = spread(keys)
    mine_col = (expert_ids == me).astype(F32)[:, None]
    key_cols = related(keys).T

    bucket_hits = (jnp.arange(BUCKETS, dtype=jnp.int32)[:, None] == buckets[None, :]).astype(BF16)
    bias_vec = lax.dot_general(bias_full, bucket_hits, (((0,), (0,)), ((), ())), preferred_element_type=F32)
    lines = bias_lines(bias_vec)
    seg_col, seg_row = segment_ids[:, None], segment_ids[None, :]

    token_rows = tokens.astype(F32)
    unit_one, inv_one, normed_one = norm_forward(token_rows, gain_one)
    act_one = normed_one.astype(BF16)
    qkv_rows = jnp.dot(act_one, qkv_weight, preferred_element_type=F32).astype(BF16)
    attended, totals = attend_forward(qkv_rows, seg_col, seg_row, lines)
    residual = token_rows + jnp.dot(attended, attn_weight, preferred_element_type=F32)
    unit_two, inv_two, normed_two = norm_forward(residual, gain_two)
    act_two = normed_two.astype(BF16)
    act_parts = spread(act_two)

    logits = lax.dot_general(router_weight, act_two, (((0,), (1,)), ((), ())), preferred_element_type=F32)
    prob_all, chosen_sum, gates = route_gates(logits, hits)

    all_pairs = [jnp.concatenate(all_keys[:2], axis=0), jnp.concatenate(all_keys[2:], axis=0)]
    router_rows = jnp.pad(router_weight.T, ((0, EXPERTS), (0, 0)))
    first = []
    for pair in range(2):
        here = slice(2 * pair, 2 * pair + 2)
        first = expert_first(
            pair, act_parts[here], cot_parts[here], all_pairs[pair], router_rows, mine_col, half_in[0], full_out, first
        )
    rows, _, dout, _, act_first, dhid_first, _, _ = first

    def weight_grad(left, right):
        return lax.dot_general(left, right, (((0,), (0,)), ((), ())), preferred_element_type=F32).astype(BF16)

    grad_in_first = weight_grad(rows, dhid_first)
    sum_in_first = sum_over_x(grad_in_first)
    far = expert_second(1, first, after(all_pairs[1], grad_in_first), mine_col, half_in[1], full_out, [])
    near = expert_second(0, first, after(all_pairs[0], sum_in_first), mine_col, half_in[1], full_out, far[:2])
    sum_in_first = sum_over_z(sum_in_first).astype(BF16)
    act_second, dhid_second = near[:2]
    dgate_parts = [swap(row, x) for x, row in enumerate([near[4][0], near[4][1], far[4][0], far[4][1]])]
    across_one = swap(far[3][:CAP], 2)
    across_two = swap(far[3][CAP:], 2)

    act_first, act_second = after((act_first, act_second), (across_one, across_two, sum_in_first))
    grad_out = jnp.concatenate([weight_grad(act_first, dout), weight_grad(act_second, dout)], axis=0)
    sum_out = lax.psum_scatter(grad_out, "shard", scatter_dimension=0, tiled=True)
    grad_in_second = weight_grad(rows, after(dhid_second, grad_out))
    in_second_x = parts_over_x(grad_in_second)

    def send_back(near_rows, across_one, across_two):
        return [near_rows[:CAP], swap(near_rows[CAP:], 1), across_one, swap(across_two, 1)]

    drow_parts = send_back(near[3], across_one, across_two)
    out_far = swap(after(far[2], across_two), 2)

    def place(values):
        if dp_size > EXPERTS:
            every = [
                jnp.sum(lax.all_gather(v, "dp", axis=0).astype(F32).reshape((-1, EXPERTS) + v.shape), axis=0)
                for v in values
            ]
            return jnp.concatenate(every, axis=2)
        parts = [jnp.concatenate(list(pieces), axis=1).astype(F32) for pieces in zip(*[spread(v) for v in values])]
        out = jnp.zeros((EXPERTS,) + parts[0].shape, F32)
        for x in range(EXPERTS):
            out = lax.dynamic_update_index_in_dim(out, parts[x], relation_ids[x], 0)
        return out

    grad_gates = related(jnp.stack(dgate_parts, axis=0))
    weighted = jnp.sum(grad_gates * gates, axis=0, keepdims=True)
    grad_prob = hits * (grad_gates - weighted) / chosen_sum
    grad_logits = (prob_all * (grad_prob - jnp.sum(prob_all * grad_prob, axis=0, keepdims=True))).astype(BF16)
    grad_router = lax.dot_general(act_two, grad_logits, (((0,), (1,)), ((), ())), preferred_element_type=F32)
    extra = lax.dot_general(grad_logits, router_weight, (((0,), (1,)), ((), ())), preferred_element_type=F32)
    grad_residual, grad_attended, grad_attn_weight, grad_gain_two = token_back(
        key_cols, extra, residual, cotangent, attended, gain_two[None], packed, drow_parts
    )
    grad_attended = after(grad_attended, grad_in_second)
    grad_split, grad_lines = attend_backward(
        qkv_rows, attended, grad_attended, totals, seg_col, seg_row, lines
    )
    grad_split, out_far, in_second_x = lax.optimization_barrier((grad_split, out_far, in_second_x))
    in_second_z = parts_over_z(add_parts(in_second_x).astype(BF16))
    grad_qkv_weight, grad_tokens, grad_gain_one = qkv_back(
        act_one, grad_split, packed, tokens, gain_one[None], grad_residual
    )
    grad_qkv_weight, sum_out = lax.optimization_barrier((grad_qkv_weight, sum_out))
    mixed_out = mix_rows(key_cols, residual, send_back(near[2], out_far[:CAP], out_far[CAP:]))
    grad_table = lax.dot_general(
        bucket_hits.astype(F32), bias_line_grads(grad_lines), (((1,), (1,)), ((), ())), precision=HIGHEST
    )
    shards = D // shard_rows
    table_sums = jnp.pad(
        grad_table.reshape(shards, table_rows * HEADS), ((0, 0), (0, shard_rows - table_rows * HEADS))
    ).reshape(D, 1)
    small = jnp.concatenate([grad_gain_one.T, grad_gain_two.T, grad_router, table_sums], axis=1)
    packed = jnp.concatenate(
        [grad_qkv_weight, grad_attn_weight, jnp.pad(small, ((0, 0), (0, 121))).astype(BF16)],
        axis=1,
    )
    packed = packed.reshape(shards, 2, core_rows, packed.shape[1])
    kept = lax.dynamic_index_in_dim(packed, core, 1, keepdims=False)
    sent = lax.dynamic_index_in_dim(packed, 1 - core, 1, keepdims=False)
    kept = (kept.astype(F32) + swap(sent, 1).astype(F32)).astype(BF16)
    kept, mixed_out, grad_tokens, in_second_z = lax.optimization_barrier(
        (sum_over_x(kept), mixed_out, grad_tokens, in_second_z)
    )
    sum_in_second = add_parts(in_second_z).astype(BF16)
    grad_w_out = place([sum_out])
    kept = sum_over_z(kept)
    grad_w_in = place([sum_in_first, sum_in_second])
    if dp_size > EXPERTS:
        total = lax.all_gather(kept, "dp", axis=0).reshape((-1, 2) + kept.shape)
        total = jnp.sum(lax.dynamic_index_in_dim(total, core, 1, keepdims=False), axis=0)
    else:
        kept = kept.astype(BF16)
        total = kept.astype(F32) + swap(kept, 2).astype(F32)
    other = swap(total, 1)
    packed = jnp.concatenate([jnp.where(core == 0, total, other), jnp.where(core == 0, other, total)], axis=0)
    return (
        mixed_out,
        grad_tokens,
        packed[:, 4 * D],
        packed[:, : 3 * D],
        packed[:, 3 * D : 4 * D],
        packed[:, 4 * D + 6][: table_rows * HEADS].reshape(table_rows, HEADS),
        packed[:, 4 * D + 1],
        packed[:, 4 * D + 2 : 4 * D + 6],
        grad_w_in,
        grad_w_out,
    )


def solution(mesh):
    return jax.shard_map(
        functools.partial(body, mesh.shape["dp"]),
        mesh=mesh,
        in_specs=(
            P(("dp", "shard"), None),
            P(("dp", "shard")),
            P(("dp", "shard"), None),
            P(),
            P("shard"),
            P("shard", None),
            P("shard", None),
            P("shard", None),
            P("shard"),
            P("shard", None),
            P(None, "shard", None),
            P(None, "shard", None),
            P(("dp", "shard"), None),
        ),
        out_specs=(
            P(("dp", "shard"), None),
            P(("dp", "shard"), None),
            P("shard"),
            P("shard", None),
            P("shard", None),
            P("shard", None),
            P("shard"),
            P("shard", None),
            P(None, "shard", None),
            P(None, "shard", None),
        ),
        check_vma=False,
    )
```

```python
import functools

import jax
import jax.numpy as jnp
from jax import lax
from jax.experimental import pallas as pl
from jax.experimental.pallas import tpu as pltpu
from jax.sharding import PartitionSpec as P

D = 768
HEADS = 12
HEAD_DIM = 64
FF = 3072
EXPERTS = 4
BUCKETS = 32
SEQ = 1024
CAP = 640
DEEP = 4
BLOCK = 256
REACH = 768
NORM_EPSILON = 1e-06
HIGHEST = lax.Precision.HIGHEST
NEG = -1e30
COST_CUT = 256
F32 = jnp.float32
BF16 = jnp.bfloat16
MIB = 1024 * 1024
GELU_ROOT = 0.7978845608028654
GELU_CUBE = 0.044715


def norm_forward(values, gain_vec):
    inv_rms = lax.rsqrt(jnp.mean(values * values, axis=-1, keepdims=True) + NORM_EPSILON)
    unit_rows = values * inv_rms
    return unit_rows, inv_rms, unit_rows * gain_vec


def cost(flops, moved):
    return pl.CostEstimate(flops=flops // COST_CUT, bytes_accessed=moved // COST_CUT, transcendentals=0)


def key_span(block):
    low = max(0, (block + 1) * BLOCK - REACH)
    return low, (block + 1) * BLOCK - low


def fill_mask(seg_col_ref, seg_row_ref, mask_ref):
    for block in range(SEQ // BLOCK):
        low, width = key_span(block)
        same = (
            seg_col_ref[low : low + width, :]
            == seg_row_ref[:, block * BLOCK : (block + 1) * BLOCK]
        )
        mask_ref[block, REACH - width :, :] = jnp.where(same, 0.0, NEG)


def fill_bias(line_ref, bias_ref):
    for head in range(2):
        for part in range(3):
            rows = line_ref[0, 3 * head + part : 3 * head + part + 1, :]
            count = 1
            while count < BLOCK:
                rows = jnp.concatenate([rows, pltpu.roll(rows, count, 1)], axis=0)
                count *= 2
            bias_ref[head, part * BLOCK : (part + 1) * BLOCK, :] = rows[:, :BLOCK]


def diagonal_sums(square):
    rows = jnp.concatenate([square, jnp.zeros_like(square)], axis=1)
    count = BLOCK
    while count > 1:
        count //= 2
        rows = rows[:count] + pltpu.roll(rows[count:], 2 * BLOCK - count, 1)
    return rows


def head_lanes(head, rows):
    lane = lax.broadcasted_iota(jnp.int32, rows.shape, 1)
    return jnp.where(lane // HEAD_DIM == head, rows, jnp.zeros_like(rows))


def dot_nt(left, right):
    return lax.dot_general(left, right, (((1,), (1,)), ((), ())), preferred_element_type=F32)


def dot_nn(left, right):
    return jnp.dot(left, right, preferred_element_type=F32)


def attention_kernel(
    q_ref, k_ref, v_ref, seg_col_ref, seg_row_ref, line_ref, out_ref, total_ref, mask_ref, bias_ref
):
    @pl.when(pl.program_id(0) == 0)
    def _():
        fill_mask(seg_col_ref, seg_row_ref, mask_ref)

    fill_bias(line_ref, bias_ref)
    values_t = v_ref[...].T
    for block in range(SEQ // BLOCK):
        low, width = key_span(block)
        here = slice(block * BLOCK, (block + 1) * BLOCK)
        queries = q_ref[here, :] * jnp.asarray(HEAD_DIM**-0.5, BF16)
        parts = []
        for head in range(2):
            scores = dot_nt(k_ref[low : low + width, :], head_lanes(head, queries))
            scores = scores + bias_ref[head, REACH - width :, :] + mask_ref[block, REACH - width :, :]
            top = jnp.max(scores, axis=0, keepdims=True)
            weights = jnp.exp(scores - top)
            denom = jnp.sum(weights, axis=0, keepdims=True)
            mixed = dot_nn(values_t[:, low : low + width], weights.astype(BF16))
            parts.append(mixed[head * HEAD_DIM : (head + 1) * HEAD_DIM, :] / denom)
            total_ref[0, head : head + 1, here] = top + jnp.log(denom)
        out_ref[here, :] = jnp.concatenate(parts, axis=0).T.astype(BF16)


def attention_back_kernel(
    q_ref, k_ref, v_ref, out_ref, grad_ref, total_ref, seg_col_ref, seg_row_ref, line_ref,
    dqkv_ref, dline_ref, mask_ref, bias_ref, dbias_ref, dk_ref, dv_ref,
):
    @pl.when(pl.program_id(0) == 0)
    def _():
        fill_mask(seg_col_ref, seg_row_ref, mask_ref)

    fill_bias(line_ref, bias_ref)
    keys_t = k_ref[...].T
    dk_ref[...] = jnp.zeros_like(dk_ref)
    dv_ref[...] = jnp.zeros_like(dv_ref)
    dbias_ref[...] = jnp.zeros_like(dbias_ref)
    scale = HEAD_DIM**-0.5
    for block in range(SEQ // BLOCK):
        low, width = key_span(block)
        here = slice(block * BLOCK, (block + 1) * BLOCK)
        span = slice(low, low + width)
        queries = q_ref[here, :] * jnp.asarray(scale, BF16)
        grads = grad_ref[here, :]
        inner = (grads.astype(F32) * out_ref[here, :].astype(F32)).T
        parts = []
        for head in range(2):
            rows = slice(head * HEAD_DIM, (head + 1) * HEAD_DIM)
            query_head = head_lanes(head, queries)
            grad_head = head_lanes(head, grads)
            scores = dot_nt(k_ref[span, :], query_head)
            scores = scores + bias_ref[head, REACH - width :, :] + mask_ref[block, REACH - width :, :]
            probs = jnp.exp(scores - total_ref[0, head : head + 1, here])
            grad_probs = dot_nt(v_ref[span, :], grad_head)
            delta = jnp.sum(inner[rows, :], axis=0, keepdims=True)
            grad_scores = probs * (grad_probs - delta)
            dbias_ref[head, REACH - width :, :] += grad_scores
            low_scores = grad_scores.astype(BF16)
            dv_ref[span, :] += dot_nn(probs.astype(BF16), grad_head)
            dk_ref[span, :] += dot_nn(low_scores, query_head)
            parts.append(dot_nn(keys_t[:, span], low_scores)[rows, :])
        dqkv_ref[0, here, :] = (jnp.concatenate(parts, axis=0).T * scale).astype(BF16)
    dqkv_ref[1, :, :] = dk_ref[...].astype(BF16)
    dqkv_ref[2, :, :] = dv_ref[...].astype(BF16)
    for head in range(2):
        for part in range(3):
            sums = diagonal_sums(dbias_ref[head, part * BLOCK : (part + 1) * BLOCK, :])
            dline_ref[0, 3 * head + part : 3 * head + part + 1, :] = sums
    dline_ref[0, 6:8, :] = jnp.zeros((2, 2 * BLOCK), F32)


def pair_spec(offset):
    return pl.BlockSpec((SEQ, 2 * HEAD_DIM), lambda pair: (0, pair + offset))


PAIRS = HEADS // 2
SEG_SPECS = [
    pl.BlockSpec((SEQ, 1), lambda pair: (0, 0)),
    pl.BlockSpec((1, SEQ), lambda pair: (0, 0)),
    pl.BlockSpec((1, 8, 2 * BLOCK), lambda pair: (pair, 0, 0)),
]
TOTAL_SPEC = pl.BlockSpec((1, 8, SEQ), lambda pair: (pair, 0, 0))
PAIR_SCRATCH = [
    pltpu.VMEM((SEQ // BLOCK, REACH, BLOCK), F32),
    pltpu.VMEM((2, REACH, BLOCK), F32),
]


def attend_forward(qkv_rows, seg_col, seg_row, lines):
    return pl.pallas_call(
        attention_kernel,
        grid=(PAIRS,),
        in_specs=[pair_spec(0), pair_spec(PAIRS), pair_spec(2 * PAIRS)] + SEG_SPECS,
        out_specs=[pair_spec(0), TOTAL_SPEC],
        out_shape=[
            jax.ShapeDtypeStruct((SEQ, D), BF16),
            jax.ShapeDtypeStruct((PAIRS, 8, SEQ), F32),
        ],
        scratch_shapes=PAIR_SCRATCH,
        compiler_params=pltpu.CompilerParams(vmem_limit_bytes=48 * MIB),
        cost_estimate=cost(4 * SEQ * SEQ * D, 8 * SEQ * D),
        name="attend_forward",
    )(qkv_rows, qkv_rows, qkv_rows, seg_col, seg_row, lines)


def attend_backward(qkv_rows, attended, grad_attended, totals, seg_col, seg_row, lines):
    return pl.pallas_call(
        attention_back_kernel,
        grid=(PAIRS,),
        in_specs=[
            pair_spec(0), pair_spec(PAIRS), pair_spec(2 * PAIRS), pair_spec(0), pair_spec(0), TOTAL_SPEC,
        ] + SEG_SPECS,
        out_specs=[
            pl.BlockSpec((3, SEQ, 2 * HEAD_DIM), lambda pair: (0, 0, pair)),
            pl.BlockSpec((1, 8, 2 * BLOCK), lambda pair: (pair, 0, 0)),
        ],
        out_shape=[
            jax.ShapeDtypeStruct((3, SEQ, D), BF16),
            jax.ShapeDtypeStruct((PAIRS, 8, 2 * BLOCK), F32),
        ],
        scratch_shapes=PAIR_SCRATCH + [
            pltpu.VMEM((2, REACH, BLOCK), F32),
            pltpu.VMEM((SEQ, 2 * HEAD_DIM), F32),
            pltpu.VMEM((SEQ, 2 * HEAD_DIM), F32),
        ],
        compiler_params=pltpu.CompilerParams(vmem_limit_bytes=48 * MIB),
        cost_estimate=cost(10 * SEQ * SEQ * D, 16 * SEQ * D),
        name="attend_backward",
    )(qkv_rows, qkv_rows, qkv_rows, attended, grad_attended, totals, seg_col, seg_row, lines)


def bias_lines(bias_vec):
    reach = jnp.concatenate([jnp.full((HEADS, BLOCK), NEG, F32), bias_vec], axis=1)
    parts = []
    for part in range(3):
        middle = REACH - part * BLOCK
        parts.append(
            jnp.concatenate([reach[:, middle : middle + BLOCK], reach[:, middle - BLOCK : middle]], axis=1)
        )
    lines = jnp.stack(parts, axis=1).reshape(PAIRS, 6, 2 * BLOCK)
    return jnp.concatenate([lines, jnp.zeros((PAIRS, 2, 2 * BLOCK), F32)], axis=1)


def bias_line_grads(grad_lines):
    parts = grad_lines[:, :6].reshape(HEADS, 3, 2 * BLOCK)
    total = jnp.zeros((HEADS, SEQ + BLOCK), F32)
    for part in range(3):
        middle = REACH - part * BLOCK
        line = jnp.concatenate([parts[:, part, BLOCK:], parts[:, part, :BLOCK]], axis=1)
        total = total + jnp.pad(line, ((0, 0), (middle - BLOCK, SEQ - middle)))
    return total[:, BLOCK:]


FF_HALF = FF // 2
FF_BLOCK = 1536
SLOTS = EXPERTS * CAP


def hidden_half(rows_ref, dout_ref, w_in_ref, w_out_ref, act_ref, dhid_ref, out_acc, drow_acc):
    def step(index, carry):
        cols = pl.ds(pl.multiple_of(index * FF_BLOCK, FF_BLOCK), FF_BLOCK)
        w_in = w_in_ref[:, cols]
        w_out = w_out_ref[cols, :]
        hidden = dot_nn(rows_ref[...], w_in)
        grad_act = dot_nt(dout_ref[...], w_out)
        square = hidden * hidden
        bend = jnp.tanh(hidden * (GELU_ROOT + (GELU_ROOT * GELU_CUBE) * square))
        half = 0.5 + 0.5 * bend
        act = (hidden * half).astype(BF16)
        slope = half + 0.5 * hidden * (1.0 - bend * bend) * (
            GELU_ROOT + (3.0 * GELU_ROOT * GELU_CUBE) * square
        )
        dhid = (grad_act * slope).astype(BF16)
        act_ref[:, cols] = act
        dhid_ref[:, cols] = dhid
        out_acc[...] += dot_nn(act, w_out)
        drow_acc[...] += dot_nt(dhid, w_in)
        return carry

    lax.fori_loop(0, FF_HALF // FF_BLOCK, step, 0)


def route_gates(logits, hits):
    shifted = jnp.exp(logits - jnp.max(logits, axis=0, keepdims=True))
    prob_all = shifted / jnp.sum(shifted, axis=0, keepdims=True)
    chosen_sum = jnp.sum(hits * prob_all, axis=0, keepdims=True)
    return prob_all, chosen_sum, hits * prob_all / chosen_sum


def pick_slots(key_row):
    slot = lax.broadcasted_iota(jnp.int32, (CAP, SEQ), 0).astype(F32)
    return key_row == slot


def first_half_kernel(
    act_one_ref, act_two_ref, cot_one_ref, cot_two_ref, key_ref, router_ref, mine_ref, w_in_ref, w_out_ref, *rest
):
    rows_ref, graw_ref, dout_ref, gcol_ref, act_ref, dhid_ref, out_acc, drow_acc = rest[-8:]

    def dispatch(index, act_part, cot_part):
        keys = key_ref[index * EXPERTS : (index + 1) * EXPERTS, :]
        logits = dot_nt(router_ref[...], act_part[...])[:EXPERTS, :]
        _, _, gate_rows = route_gates(logits, jnp.where(keys >= 0.0, 1.0, 0.0))
        mine = mine_ref[...] > 0.0
        picks = pick_slots(jnp.sum(jnp.where(mine, keys, 0.0), axis=0, keepdims=True))
        gate_row = jnp.sum(jnp.where(mine, gate_rows, 0.0), axis=0, keepdims=True)
        gates = jnp.sum(jnp.where(picks, gate_row, 0.0), axis=1, keepdims=True)
        chosen = jnp.where(picks, 1.0, 0.0).astype(BF16)
        rows_ref[...] = dot_nn(chosen, act_part[...]).astype(BF16)
        grads = dot_nn(chosen, cot_part[...])
        graw_ref[...] = grads.astype(BF16)
        dout_ref[...] = (gates * grads).astype(BF16)
        gcol_ref[...] = gates

    @pl.when(pl.program_id(0) == 0)
    def _():
        dispatch(0, act_one_ref, cot_one_ref)

    @pl.when(pl.program_id(0) == 1)
    def _():
        dispatch(1, act_two_ref, cot_two_ref)

    out_acc[...] = jnp.zeros_like(out_acc)
    drow_acc[...] = jnp.zeros_like(drow_acc)
    hidden_half(rows_ref, dout_ref, w_in_ref, w_out_ref, act_ref, dhid_ref, out_acc, drow_acc)


def second_half_kernel(
    rows_ref, graw_ref, dout_ref, gcol_ref, out_in, drow_in, key_ref, mine_ref, w_in_ref, w_out_ref, *rest
):
    act_ref, dhid_ref, out_ref, drow_ref, dgate_ref, out_acc, drow_acc = rest[-7:]
    out_acc[...] = out_in[...]
    drow_acc[...] = drow_in[...]
    hidden_half(rows_ref, dout_ref, w_in_ref, w_out_ref, act_ref, dhid_ref, out_acc, drow_acc)
    outs = out_acc[...]
    out_ref[...] = (gcol_ref[...] * outs).astype(BF16)
    drow_ref[...] = drow_acc[...].astype(BF16)
    dgates = jnp.sum(graw_ref[...].astype(F32) * outs, axis=1, keepdims=True)
    for index in range(2):

        @pl.when(pl.program_id(0) == index)
        def _():
            keys = key_ref[index * EXPERTS : (index + 1) * EXPERTS, :]
            picks = pick_slots(jnp.sum(jnp.where(mine_ref[...] > 0.0, keys, 0.0), axis=0, keepdims=True))
            dgate_ref[index : index + 1, :] = jnp.sum(jnp.where(picks, dgates, 0.0), axis=0, keepdims=True)


ANY_SPEC = pl.BlockSpec(memory_space=pl.ANY)


def place_kernel(order_ref, *refs):
    out_ref = refs[-1]
    for index, block in enumerate(refs[:-1]):
        out_ref[order_ref[index]] = block[...]


def place_blocks(order, blocks):
    shape = blocks[0].shape
    vmem = pl.BlockSpec(memory_space=pltpu.VMEM)
    return pl.pallas_call(
        place_kernel,
        in_specs=[pl.BlockSpec(memory_space=pltpu.SMEM)] + [vmem] * len(blocks),
        out_specs=vmem,
        out_shape=jax.ShapeDtypeStruct((len(blocks),) + shape, blocks[0].dtype),
        compiler_params=pltpu.CompilerParams(vmem_limit_bytes=32 * MIB),
        cost_estimate=cost(0, 4 * len(blocks) * shape[0] * shape[1]),
        name="place_blocks",
    )(order, *blocks)


ROW_BLOCK = 256


def picked_sum(key_ref, parts):
    slot = lax.broadcasted_iota(jnp.int32, (ROW_BLOCK, CAP), 1).astype(F32)
    total = None
    for index, part in enumerate(parts):
        picks = jnp.where(key_ref[:, index : index + 1] == slot, 1.0, 0.0).astype(BF16)
        rows = dot_nn(picks, part[...])
        total = rows if total is None else total + rows
    return total


def mix_kernel(key_ref, base_ref, one_ref, two_ref, three_ref, four_ref, out_ref):
    total = picked_sum(key_ref, (one_ref, two_ref, three_ref, four_ref))
    out_ref[...] = (base_ref[...] + total).astype(BF16)


def row_spec(width):
    return pl.BlockSpec((ROW_BLOCK, width), lambda step: (step, 0))


def mix_rows(keys, base, parts):
    return pl.pallas_call(
        mix_kernel,
        grid=(SEQ // ROW_BLOCK,),
        in_specs=[row_spec(EXPERTS), row_spec(D)] + [fixed_spec((CAP, D))] * EXPERTS,
        out_specs=row_spec(D),
        out_shape=jax.ShapeDtypeStruct((SEQ, D), BF16),
        compiler_params=pltpu.CompilerParams(vmem_limit_bytes=32 * MIB),
        cost_estimate=cost(2 * SEQ * SLOTS * D, 2 * SLOTS * D + 6 * SEQ * D),
        name="mix_rows",
    )(keys, base, *parts)


def norm_back(values, grad_norm, gain):
    inv_rms = lax.rsqrt(jnp.mean(values * values, axis=-1, keepdims=True) + NORM_EPSILON)
    unit_rows = values * inv_rms
    grad_gain = jnp.sum(grad_norm * unit_rows, axis=0, keepdims=True)
    grad_unit = grad_norm * gain
    middle = jnp.mean(grad_unit * unit_rows, axis=-1, keepdims=True)
    return inv_rms * (grad_unit - unit_rows * middle), grad_gain


def token_back_kernel(
    key_ref, extra_ref, residual_ref, cot_ref, attended_ref, gain_ref, weight_ref,
    one_ref, two_ref, three_ref, four_ref,
    grad_ref, dattended_ref, dweight_ref, dgain_ref, dweight_acc,
):
    step = pl.program_id(0)

    @pl.when(step == 0)
    def _():
        dweight_acc[...] = jnp.zeros_like(dweight_acc)
        dgain_ref[...] = jnp.zeros_like(dgain_ref)

    grad_act = extra_ref[...] + picked_sum(key_ref, (one_ref, two_ref, three_ref, four_ref))
    grad_norm, grad_gain = norm_back(residual_ref[...], grad_act, gain_ref[...])
    grad_rows = cot_ref[...].astype(F32) + grad_norm
    grad_ref[...] = grad_rows
    dgain_ref[...] += grad_gain
    branch = grad_rows.astype(BF16)
    dattended_ref[...] = dot_nt(branch, weight_ref[...]).astype(BF16)
    dweight_acc[...] += lax.dot_general(
        attended_ref[...], branch, (((0,), (0,)), ((), ())), preferred_element_type=F32
    )

    @pl.when(step == SEQ // ROW_BLOCK - 1)
    def _():
        dweight_ref[...] = dweight_acc[...].astype(BF16)


def token_back(keys, extra, residual, cotangent, attended, gain, packed, parts):
    return pl.pallas_call(
        token_back_kernel,
        grid=(SEQ // ROW_BLOCK,),
        in_specs=[row_spec(EXPERTS), row_spec(D), row_spec(D), row_spec(D), row_spec(D)]
        + [fixed_spec((1, D)), pl.BlockSpec((D, D), lambda step: (0, 3), pipeline_mode=pl.Buffered(1))]
        + [fixed_spec((CAP, D))] * EXPERTS,
        out_specs=[row_spec(D), row_spec(D), fixed_spec((D, D)), fixed_spec((1, D))],
        out_shape=[
            jax.ShapeDtypeStruct((SEQ, D), F32),
            jax.ShapeDtypeStruct((SEQ, D), BF16),
            jax.ShapeDtypeStruct((D, D), BF16),
            jax.ShapeDtypeStruct((1, D), F32),
        ],
        scratch_shapes=[pltpu.VMEM((D, D), F32)],
        compiler_params=pltpu.CompilerParams(vmem_limit_bytes=40 * MIB),
        cost_estimate=cost(2 * SEQ * (SLOTS + 2 * D) * D, 2 * SLOTS * D + 18 * SEQ * D),
        name="token_back",
    )(keys, extra, residual, cotangent, attended, gain, packed, *parts)


def qkv_back_kernel(
    act_ref, split_ref, weight_ref, token_ref, gain_ref, grad_ref,
    dweight_ref, dtoken_ref, dgain_ref, act_t, total,
):
    step = pl.program_id(0)

    @pl.when(step == 0)
    def _():
        act_t[...] = act_ref[...].T
        total[...] = jnp.zeros_like(total)

    split = split_ref[0]
    dweight_ref[...] = dot_nn(act_t[...], split).astype(BF16)
    total[...] += dot_nt(split, weight_ref[...])

    @pl.when(step == 2)
    def _():
        grad_norm, grad_gain = norm_back(token_ref[...].astype(F32), total[...], gain_ref[...])
        dtoken_ref[...] = (grad_ref[...] + grad_norm).astype(BF16)
        dgain_ref[...] = grad_gain


def qkv_back(act_one, grad_split, packed, tokens, gain, grad_residual):
    return pl.pallas_call(
        qkv_back_kernel,
        grid=(3,),
        in_specs=[
            fixed_spec((SEQ, D)),
            pl.BlockSpec((1, SEQ, D), lambda step: (step, 0, 0)),
            pl.BlockSpec((D, D), lambda step: (0, step)),
            fixed_spec((SEQ, D)),
            fixed_spec((1, D)),
            fixed_spec((SEQ, D)),
        ],
        out_specs=[pl.BlockSpec((D, D), lambda step: (0, step)), fixed_spec((SEQ, D)), fixed_spec((1, D))],
        out_shape=[
            jax.ShapeDtypeStruct((D, 3 * D), BF16),
            jax.ShapeDtypeStruct((SEQ, D), BF16),
            jax.ShapeDtypeStruct((1, D), F32),
        ],
        scratch_shapes=[pltpu.VMEM((D, SEQ), BF16), pltpu.VMEM((SEQ, D), F32)],
        compiler_params=pltpu.CompilerParams(vmem_limit_bytes=48 * MIB),
        cost_estimate=cost(12 * SEQ * D * D, 16 * SEQ * D + 12 * D * D),
        name="qkv_back",
    )(act_one, grad_split, packed, tokens, gain, grad_residual)


def slot_spec(pair, width):
    return pl.BlockSpec((CAP, width), lambda step: (2 * pair + step, 0))


def fixed_spec(shape, row=0):
    return pl.BlockSpec(shape, lambda step: (row, 0), pipeline_mode=pl.Buffered(1))


def expert_cost():
    return cost(16 * CAP * D * FF_HALF, 4 * D * FF_HALF + 20 * CAP * D)


def expert_first(pair, acts, cots, keys, router_rows, mine, w_in, w_out, earlier):
    widths = [(D, BF16), (D, BF16), (D, BF16), (1, F32), (FF_HALF, BF16), (FF_HALF, BF16), (D, F32), (D, F32)]
    inputs = [acts[0], acts[1], cots[0], cots[1], keys, router_rows, mine, w_in, w_out]
    return pl.pallas_call(
        first_half_kernel,
        grid=(2,),
        in_specs=[fixed_spec((SEQ, D))] * 4
        + [fixed_spec((2 * EXPERTS, SEQ)), fixed_spec((2 * EXPERTS, D)), fixed_spec((EXPERTS, 1))]
        + [fixed_spec((D, FF_HALF)), fixed_spec((FF_HALF, D))]
        + [ANY_SPEC] * len(earlier),
        out_specs=[slot_spec(pair, width) for width, _ in widths],
        out_shape=[jax.ShapeDtypeStruct((SLOTS, width), kind) for width, kind in widths],
        input_output_aliases={len(inputs) + i: i for i in range(len(earlier))},
        compiler_params=pltpu.CompilerParams(vmem_limit_bytes=56 * MIB),
        cost_estimate=expert_cost(),
        name="expert_first",
    )(*inputs, *earlier)


def expert_second(pair, first, keys, mine, w_in, w_out, earlier):
    rows, graw, dout, gcol, _, _, outs, drows = first
    wide = jax.ShapeDtypeStruct((SLOTS, FF_HALF), BF16)
    narrow = jax.ShapeDtypeStruct((2 * CAP, D), BF16)
    inputs = [rows, graw, dout, gcol, outs, drows, keys, mine, w_in, w_out]
    return pl.pallas_call(
        second_half_kernel,
        grid=(2,),
        in_specs=[slot_spec(pair, width) for width in (D, D, D, 1, D, D)]
        + [fixed_spec((2 * EXPERTS, SEQ)), fixed_spec((EXPERTS, 1))]
        + [fixed_spec((D, FF_HALF)), fixed_spec((FF_HALF, D), 1)]
        + [ANY_SPEC] * len(earlier),
        out_specs=[slot_spec(pair, FF_HALF)] * 2 + [slot_spec(0, D)] * 2 + [fixed_spec((8, SEQ))],
        out_shape=[wide, wide, narrow, narrow, jax.ShapeDtypeStruct((8, SEQ), F32)],
        input_output_aliases={len(inputs) + i: i for i in range(len(earlier))},
        scratch_shapes=[pltpu.VMEM((CAP, D), F32), pltpu.VMEM((CAP, D), F32)],
        compiler_params=pltpu.CompilerParams(vmem_limit_bytes=56 * MIB),
        cost_estimate=expert_cost(),
        name="expert_second",
    )(*inputs, *earlier)


def body(
    dp_size, tokens, segment_ids, routes, buckets, norm1_gain, w_qkv, w_attn_out, bias_table,
    norm2_gain, router, w_in, w_expert_out, cotangent,
):
    shard_rows = w_qkv.shape[0]
    table_rows = bias_table.shape[0]
    me = lax.axis_index("dp") % EXPERTS

    def swap(value, relation):
        if relation == 0:
            return value
        return lax.ppermute(value, "dp", [(i, i ^ relation) for i in range(dp_size)])

    across_x = (D // shard_rows) // DEEP
    shard_id = lax.axis_index("shard")
    my_z, my_x = shard_id // across_x, shard_id % across_x

    def step_z(value, step):
        pairs = [
            (z * across_x + x, (z + step) % DEEP * across_x + x) for z in range(DEEP) for x in range(across_x)
        ]
        return lax.ppermute(value, "shard", pairs)

    def step_x(value, step):
        pairs = [
            (z * across_x + x, z * across_x + (x + step) % across_x) for z in range(DEEP) for x in range(across_x)
        ]
        return lax.ppermute(value, "shard", pairs)

    def gather_rows(value):
        pieces = {}
        for back in range(DEEP):
            pieces[back, 0] = value if back == 0 else step_z(value, back)
            for side in range(1, across_x):
                pieces[back, side] = step_x(pieces[back, 0], side)
        order, blocks = [], []
        for (back, side), block in pieces.items():
            order.append((my_z - back) % DEEP * across_x + (my_x - side) % across_x)
            blocks.append(block)
        return place_blocks(jnp.stack(order).astype(jnp.int32), blocks)

    def parts_over_x(value):
        value = value.reshape(DEEP, across_x, -1, value.shape[-1])
        parts = [lax.dynamic_index_in_dim(value, my_x, 1, keepdims=False)]
        for step in range(1, across_x):
            sent = lax.dynamic_index_in_dim(value, (my_x + step) % across_x, 1, keepdims=False)
            parts.append(step_x(sent, step))
        return parts

    def parts_over_z(value):
        parts = [lax.dynamic_index_in_dim(value, my_z, 0, keepdims=False)]
        for step in range(1, DEEP):
            sent = lax.dynamic_index_in_dim(value, (my_z + step) % DEEP, 0, keepdims=False)
            parts.append(step_z(sent, step))
        return parts

    def add_parts(parts):
        total = parts[0].astype(F32)
        for part in parts[1:]:
            total = total + part.astype(F32)
        return total

    def sum_over_x(value):
        return add_parts(parts_over_x(value)).astype(BF16)

    def sum_over_z(value):
        return add_parts(parts_over_z(value))

    def after(values, earlier):
        return lax.optimization_barrier((values, earlier))[0]

    def spread(value):
        across = swap(value, 2)
        return [value, swap(value, 1), across, swap(across, 1)]

    table_col = jnp.pad(bias_table.reshape(-1), (0, shard_rows - table_rows * HEADS))
    small = jnp.concatenate(
        [norm1_gain[:, None], norm2_gain[:, None], router, table_col[:, None]], axis=1
    )
    packed = jnp.concatenate([w_qkv, w_attn_out, jnp.pad(small, ((0, 0), (0, 121)))], axis=1)
    core = lax.axis_index("dp") % 2
    core_rows = shard_rows // 2
    mine = lax.dynamic_slice_in_dim(packed, core * core_rows, core_rows, 0)
    mine = gather_rows(mine)
    other = swap(mine, 1)
    first_rows = jnp.where(core == 0, mine, other)[:, None]
    last_rows = jnp.where(core == 0, other, mine)[:, None]
    packed = jnp.concatenate([first_rows, last_rows], axis=1).reshape(D, mine.shape[2])
    qkv_weight = packed[:, : 3 * D]
    attn_weight = packed[:, 3 * D : 4 * D]
    gain_one = packed[:, 4 * D].astype(F32)
    gain_two = packed[:, 4 * D + 1].astype(F32)
    router_weight = packed[:, 4 * D + 2 : 4 * D + 6]
    bias_full = packed[:, 4 * D + 6].reshape(-1, shard_rows)[:, : table_rows * HEADS].reshape(BUCKETS, HEADS)

    my_in = lax.dynamic_index_in_dim(w_in, me, 0, keepdims=False)
    my_out = lax.dynamic_index_in_dim(w_expert_out, me, 0, keepdims=False)
    half_in = [lax.all_gather(my_in[:, :FF_HALF], "shard", axis=0, tiled=True)]
    full_out = lax.all_gather(my_out, "shard", axis=0, tiled=True)
    half_in.append(lax.all_gather(my_in[:, FF_HALF:], "shard", axis=0, tiled=True))

    cot_parts = spread(cotangent)

    expert_ids = jnp.arange(EXPERTS, dtype=jnp.int32)
    hits = (
        (routes[:, 0][None, :] == expert_ids[:, None]) | (routes[:, 1][None, :] == expert_ids[:, None])
    ).astype(F32)
    token_ids = jnp.arange(SEQ, dtype=jnp.int32)
    before = (token_ids[:, None] < token_ids[None, :]).astype(BF16)
    places = jnp.dot(hits.astype(BF16), before, preferred_element_type=F32)
    keys = jnp.where(hits > 0, places, -1.0)
    relation_ids = me ^ expert_ids

    def related(rows):
        chosen = (relation_ids[:, None] == expert_ids[None, :]).astype(F32)
        return jnp.sum(chosen[:, :, None] * rows[None], axis=1)

    all_keys = spread(keys)
    mine_col = (expert_ids == me).astype(F32)[:, None]
    key_cols = related(keys).T

    bucket_hits = (jnp.arange(BUCKETS, dtype=jnp.int32)[:, None] == buckets[None, :]).astype(BF16)
    bias_vec = lax.dot_general(bias_full, bucket_hits, (((0,), (0,)), ((), ())), preferred_element_type=F32)
    lines = bias_lines(bias_vec)
    seg_col, seg_row = segment_ids[:, None], segment_ids[None, :]

    token_rows = tokens.astype(F32)
    unit_one, inv_one, normed_one = norm_forward(token_rows, gain_one)
    act_one = normed_one.astype(BF16)
    qkv_rows = jnp.dot(act_one, qkv_weight, preferred_element_type=F32).astype(BF16)
    attended, totals = attend_forward(qkv_rows, seg_col, seg_row, lines)
    residual = token_rows + jnp.dot(attended, attn_weight, preferred_element_type=F32)
    unit_two, inv_two, normed_two = norm_forward(residual, gain_two)
    act_two = normed_two.astype(BF16)
    act_parts = spread(act_two)

    logits = lax.dot_general(router_weight, act_two, (((0,), (1,)), ((), ())), preferred_element_type=F32)
    prob_all, chosen_sum, gates = route_gates(logits, hits)

    all_pairs = [jnp.concatenate(all_keys[:2], axis=0), jnp.concatenate(all_keys[2:], axis=0)]
    router_rows = jnp.pad(router_weight.T, ((0, EXPERTS), (0, 0)))
    first = []
    for pair in range(2):
        here = slice(2 * pair, 2 * pair + 2)
        first = expert_first(
            pair, act_parts[here], cot_parts[here], all_pairs[pair], router_rows, mine_col, half_in[0], full_out, first
        )
    rows, _, dout, _, act_first, dhid_first, _, _ = first

    def weight_grad(left, right):
        return lax.dot_general(left, right, (((0,), (0,)), ((), ())), preferred_element_type=F32).astype(BF16)

    grad_in_first = weight_grad(rows, dhid_first)
    sum_in_first = sum_over_x(grad_in_first)
    far = expert_second(1, first, after(all_pairs[1], grad_in_first), mine_col, half_in[1], full_out, [])
    near = expert_second(0, first, after(all_pairs[0], sum_in_first), mine_col, half_in[1], full_out, far[:2])
    in_first_z = parts_over_z(sum_in_first)
    act_second, dhid_second = near[:2]
    dgate_parts = [swap(row, x) for x, row in enumerate([near[4][0], near[4][1], far[4][0], far[4][1]])]
    across_one = swap(far[3][:CAP], 2)
    across_two = swap(far[3][CAP:], 2)

    act_first, act_second, across_one, across_two, in_first_z = lax.optimization_barrier(
        (act_first, act_second, across_one, across_two, in_first_z)
    )
    sum_in_first = add_parts(in_first_z).astype(BF16)
    grad_out = jnp.concatenate([weight_grad(act_first, dout), weight_grad(act_second, dout)], axis=0)
    sum_out = lax.psum_scatter(grad_out, "shard", scatter_dimension=0, tiled=True)
    grad_in_second = weight_grad(rows, after(dhid_second, grad_out))
    in_second_x = parts_over_x(grad_in_second)

    def send_back(near_rows, across_one, across_two):
        return [near_rows[:CAP], swap(near_rows[CAP:], 1), across_one, swap(across_two, 1)]

    drow_parts = send_back(near[3], across_one, across_two)
    out_far = swap(after(far[2], across_two), 2)

    def place(values):
        if dp_size > EXPERTS:
            every = [
                jnp.sum(lax.all_gather(v, "dp", axis=0).astype(F32).reshape((-1, EXPERTS) + v.shape), axis=0)
                for v in values
            ]
            return jnp.concatenate(every, axis=2)
        parts = [jnp.concatenate(list(pieces), axis=1).astype(F32) for pieces in zip(*[spread(v) for v in values])]
        out = jnp.zeros((EXPERTS,) + parts[0].shape, F32)
        for x in range(EXPERTS):
            out = lax.dynamic_update_index_in_dim(out, parts[x], relation_ids[x], 0)
        return out

    grad_gates = related(jnp.stack(dgate_parts, axis=0))
    weighted = jnp.sum(grad_gates * gates, axis=0, keepdims=True)
    grad_prob = hits * (grad_gates - weighted) / chosen_sum
    grad_logits = (prob_all * (grad_prob - jnp.sum(prob_all * grad_prob, axis=0, keepdims=True))).astype(BF16)
    grad_router = lax.dot_general(act_two, grad_logits, (((0,), (1,)), ((), ())), preferred_element_type=F32)
    extra = lax.dot_general(grad_logits, router_weight, (((0,), (1,)), ((), ())), preferred_element_type=F32)
    grad_residual, grad_attended, grad_attn_weight, grad_gain_two = token_back(
        key_cols, extra, residual, cotangent, attended, gain_two[None], packed, drow_parts
    )
    grad_attended = after(grad_attended, grad_in_second)
    grad_split, grad_lines = attend_backward(
        qkv_rows, attended, grad_attended, totals, seg_col, seg_row, lines
    )
    grad_split, out_far, in_second_x = lax.optimization_barrier((grad_split, out_far, in_second_x))
    in_second_z = parts_over_z(add_parts(in_second_x).astype(BF16))
    grad_qkv_weight, grad_tokens, grad_gain_one = qkv_back(
        act_one, grad_split, packed, tokens, gain_one[None], grad_residual
    )
    mixed_out = mix_rows(key_cols, residual, send_back(near[2], out_far[:CAP], out_far[CAP:]))
    grad_table = lax.dot_general(
        bucket_hits.astype(F32), bias_line_grads(grad_lines), (((1,), (1,)), ((), ())), precision=HIGHEST
    )
    shards = D // shard_rows
    table_sums = jnp.pad(
        grad_table.reshape(shards, table_rows * HEADS), ((0, 0), (0, shard_rows - table_rows * HEADS))
    ).reshape(D, 1)
    small = jnp.concatenate([grad_gain_one.T, grad_gain_two.T, grad_router, table_sums], axis=1)
    packed = jnp.concatenate(
        [grad_qkv_weight, grad_attn_weight, jnp.pad(small, ((0, 0), (0, 121))).astype(BF16)],
        axis=1,
    )
    packed, sum_out = lax.optimization_barrier((packed, sum_out))
    packed = packed.reshape(shards, 2, core_rows, packed.shape[1])
    kept = lax.dynamic_index_in_dim(packed, core, 1, keepdims=False)
    sent = lax.dynamic_index_in_dim(packed, 1 - core, 1, keepdims=False)
    kept = (kept.astype(F32) + swap(sent, 1).astype(F32)).astype(BF16)
    kept, mixed_out, grad_tokens, in_second_z = lax.optimization_barrier(
        (sum_over_x(kept), mixed_out, grad_tokens, in_second_z)
    )
    sum_in_second = add_parts(in_second_z).astype(BF16)
    grad_w_out = place([sum_out])
    kept = sum_over_z(kept)
    grad_w_in = place([sum_in_first, sum_in_second])
    if dp_size > EXPERTS:
        total = lax.all_gather(kept, "dp", axis=0).reshape((-1, 2) + kept.shape)
        total = jnp.sum(lax.dynamic_index_in_dim(total, core, 1, keepdims=False), axis=0)
    else:
        kept = kept.astype(BF16)
        total = kept.astype(F32) + swap(kept, 2).astype(F32)
    other = swap(total, 1)
    packed = jnp.concatenate([jnp.where(core == 0, total, other), jnp.where(core == 0, other, total)], axis=0)
    return (
        mixed_out,
        grad_tokens,
        packed[:, 4 * D],
        packed[:, : 3 * D],
        packed[:, 3 * D : 4 * D],
        packed[:, 4 * D + 6][: table_rows * HEADS].reshape(table_rows, HEADS),
        packed[:, 4 * D + 1],
        packed[:, 4 * D + 2 : 4 * D + 6],
        grad_w_in,
        grad_w_out,
    )


def solution(mesh):
    return jax.shard_map(
        functools.partial(body, mesh.shape["dp"]),
        mesh=mesh,
        in_specs=(
            P(("dp", "shard"), None),
            P(("dp", "shard")),
            P(("dp", "shard"), None),
            P(),
            P("shard"),
            P("shard", None),
            P("shard", None),
            P("shard", None),
            P("shard"),
            P("shard", None),
            P(None, "shard", None),
            P(None, "shard", None),
            P(("dp", "shard"), None),
        ),
        out_specs=(
            P(("dp", "shard"), None),
            P(("dp", "shard"), None),
            P("shard"),
            P("shard", None),
            P("shard", None),
            P("shard", None),
            P("shard"),
            P("shard", None),
            P(None, "shard", None),
            P(None, "shard", None),
        ),
        check_vma=False,
    )
```
